128 devices in a mesh: tile: 16 (over y, z), chan: 8 (over x, core).
Axes of the slice: x: 4, y: 4, z: 4, core: 2. Of those that a mesh axis runs over, the one named last changes fastest.
Arguments:
- grid: bfloat16 [512, 256, 256], P('chan', 'tile'), may hold values from -6 to 6
- station_feats: bfloat16 [512, 8192], P('chan', 'tile'), may hold values from -6 to 6
- owner_tile: int32 [8192, 1], P('tile'), may hold values from 0 to 15; in each aligned block of 512 rows (0 to 511, 512 to 1023, ...) at most 64 rows name the same one
- station_cell: int32 [8192], P('tile'), may hold values from 0 to 4095
- valid: int32 [8192], P('tile'), may hold values 0 or 1
- conv_first: bfloat16 [3, 3, 512, 512], P(None, None, None, 'chan'), may hold values from -0.09375 to 0.09375
- conv_second: bfloat16 [3, 3, 512, 512], P(None, None, None, 'chan'), may hold values from -0.09375 to 0.09375
- grad_out: bfloat16 [512, 256, 256], P('chan', 'tile'), may hold values from -6 to 6
Outputs:
- output: bfloat16 [512, 256, 256], P('chan', 'tile')
- grad_weight: bfloat16 [3, 3, 512, 512], P(None, None, 'tile', 'chan')
- grad_hidden: bfloat16 [512, 256, 256], P('chan', 'tile')
The draws below stay inside these ranges and needn't reach their ends.
Inputs may be any that keep to these rules, and one draw needn't show every extreme that they name: `owner_tile`: among the 512 rows of one tile shard, at most 64 name one tile.
All inputs are finite; a program needn't handle non-finite values. No bound on the sum of `valid` on one device may be relied on, other than what follows from the above.
Results may differ from the reference program's by a relative error of at most 0.0051.
Values may be sent and summed in bfloat16 or wider, within the bound.
A program may use at most 128 MiB of HBM per device.

```python
import math
import jax
import jax.numpy as jnp
import numpy as np

C = 512
H_DEV = 16
W = 256
S_DEV = 512
CAP = 64
HEIGHT = 256
CELLS = 4096
STATIONS = 8192
N_TILE = 16


def plant(result, key, low, largest):
    dims = result.shape
    index_at = [jax.random.randint(jax.random.fold_in(key, axis), (), 0, dims[axis]) for axis in range(len(dims))]
    result = result.at[tuple(index_at)].set(low)
    longest = dims.index(max(dims))
    index_at[longest] = (index_at[longest] + 1) % dims[longest]
    return result.at[tuple(index_at)].set(largest)


def block_scale(rng, dims, shards, least, high):
    loudness = 1.0
    for position, shards_of in shards:
        heights = jax.random.uniform(jax.random.fold_in(jax.random.fold_in(rng, 6), position), (shards_of,), jnp.float32, least / len(shards), high / len(shards))
        loudness = loudness * jnp.repeat(jnp.exp(heights), dims[position] // shards_of).reshape((-1,) + (1,) * (len(dims) - 1 - position))
    return loudness


def deal_out(rng, own, number, rows, count, top, reach, lean):
    sequence = jax.random.permutation(rng, count)
    crowded, common = portions_of(count, rows * top, reach, lean, True), portions_of(count, rows * top, reach, lean, False)
    places = jnp.arange(count)

    def named(tallies, rotation):
        used = int((tallies > 0).sum())
        fixed = max(1, used // 4)
        passed = fixed + (places - fixed + rotation * (used - fixed)) % max(1, count - fixed)
        return jnp.zeros((count,), jnp.int32).at[sequence[jnp.where(places < fixed, places, passed)]].set(jnp.asarray(tallies, jnp.int32))

    tallies = jnp.where(number % 4 == 0, named(crowded, number // 4), named(common, number - number // 4 - 1))
    mixed = jax.random.permutation(jax.random.fold_in(own, 3), count)
    source_of, taker = mixed[0:count // 2 * 2:2], mixed[1:count // 2 * 2:2]
    margin = jnp.minimum(tallies[source_of] - 1, reach - tallies[taker]) // 2
    margin = jnp.where((source_of == sequence[0]) | (taker == sequence[0]) | (tallies[taker] == 0), 0, jnp.maximum(margin, 0))
    passed = jax.random.randint(jax.random.fold_in(own, 4), (count // 2,), 0, 1 << 20) % (margin + 1)
    tallies = tallies.at[source_of].add(-passed).at[taker].add(passed)
    labels = jnp.searchsorted(jnp.cumsum(tallies), jnp.arange(rows * top), side="right").astype(jnp.int32)
    table = labels.reshape(top, rows).T
    table = table[jax.random.permutation(jax.random.fold_in(own, 1), rows)]
    rotation = jax.random.randint(jax.random.fold_in(own, 2), (rows, 1), 0, top)
    return jnp.take_along_axis(table, (jnp.arange(top)[None, :] + rotation) % top, axis=1)


def portions_of(count, total, limit, lean, full):
    portions = [(1 << 20) // math.isqrt(standing ** lean) + 1 for standing in range(1, count + 1)]
    largest = limit if full else min(limit, max(-(-total // count), total * portions[0] // sum(portions)))
    least = 1 if total - largest >= count - 1 else 0
    given, spare = [largest] + [least] * (count - 1), total - largest - least * (count - 1)
    while spare > 0:
        free = [i for i in range(1, count) if given[i] < largest] or [i for i in range(1, count) if given[i] < limit]
        mass, remaining = sum([portions[i] for i in free]), spare
        for i in free:
            extra = min(limit - given[i], max(1, remaining * portions[i] // mass), spare)
            given[i] = given[i] + extra
            spare = spare - extra
    return np.array(given)


def bell_draw(rng, extent, deviation, limit, shards=(), dtype=jnp.bfloat16):
    level = block_scale(rng, extent, shards, -0.22, 0.18) if shards else 1.0
    array = jax.random.normal(rng, extent, jnp.float32) * deviation * level
    return jnp.minimum(jnp.maximum(array, -limit), limit).astype(dtype)


def setup_inputs(seed: int = 0) -> dict:
    keys = jax.random.split(jax.random.key(seed), 9)
    grid = bell_draw(keys[0], (C, HEIGHT, W), 1.0, 6.0, ((0, 8), (1, 16)))
    station_feats = bell_draw(keys[1], (C, STATIONS), 1.0, 6.0, ((0, 8), (1, 16)))
    owner_tile_keys = jax.random.split(jax.random.fold_in(keys[2], 1), STATIONS // S_DEV)
    owner_tile_turns = jax.random.permutation(jax.random.fold_in(keys[2], 3), STATIONS // S_DEV)
    owner_tile = jax.vmap(lambda own, number: deal_out(jax.random.fold_in(keys[2], 2), own, number, S_DEV, N_TILE, 1, CAP, 2))(owner_tile_keys, owner_tile_turns).reshape((STATIONS, 1))
    station_cell = plant(jax.random.randint(keys[3], (STATIONS,), 0, CELLS), jax.random.fold_in(keys[3], 1), 0, CELLS - 1).astype(jnp.int32)
    valid = plant((jax.random.randint(keys[4], (STATIONS,), 0, 4) < 3).astype(jnp.int32), jax.random.fold_in(keys[4], 1), 0, 1)
    conv_first = bell_draw(keys[5], (3, 3, C, C), (9 * C) ** -0.5, 0.09375, ((3, 8),))
    conv_second = bell_draw(keys[6], (3, 3, C, C), (9 * C) ** -0.5, 0.09375, ((3, 8),))
    grad_out = bell_draw(keys[7], (C, HEIGHT, W), 1.0, 6.0, ((0, 8), (1, 16)))
    return {"grid": grid, "station_feats": station_feats, "owner_tile": owner_tile, "station_cell": station_cell, "valid": valid, "conv_first": conv_first, "conv_second": conv_second, "grad_out": grad_out}


def convolve(source, weights, height, width):
    padded = jnp.pad(source.astype(jnp.float32), ((0, 0), (1, 1), (1, 1)))
    summed = jnp.zeros((weights.shape[3], height, width), jnp.float32)
    for row_off in range(3):
        for col_off in range(3):
            window = padded[:, row_off:row_off + height, col_off:col_off + width]
            summed = summed + jnp.einsum("chw,co->ohw", window, weights[row_off, col_off].astype(jnp.float32))
    return summed


def reference(grid, station_feats, owner_tile, station_cell, valid, conv_first, conv_second, grad_out):
    channels, height, width = grid.shape
    cell_count = H_DEV * W
    flat_index = (owner_tile[:, 0] * cell_count + station_cell).astype(jnp.int32)
    weighted = station_feats.astype(jnp.float32) * valid.astype(jnp.float32)[None, :]
    station_sum = jnp.zeros((channels, height * width), jnp.float32).at[:, flat_index].add(weighted)
    assimilated = (grid.astype(jnp.float32) + station_sum.reshape(channels, height, width)).astype(jnp.bfloat16)
    hidden_pre = convolve(assimilated, conv_first, height, width)
    hidden = jax.nn.silu(hidden_pre).astype(jnp.bfloat16)
    output = (assimilated.astype(jnp.float32) + convolve(hidden, conv_second, height, width)).astype(jnp.bfloat16)
    padded_hidden = jnp.pad(hidden.astype(jnp.float32), ((0, 0), (1, 1), (1, 1)))
    cotangent = grad_out.astype(jnp.float32)
    grad_rows = []
    for row_off in range(3):
        for col_off in range(3):
            window = padded_hidden[:, row_off:row_off + height, col_off:col_off + width]
            grad_rows.append(jnp.einsum("chw,ohw->co", window, cotangent))
    grad_weight = jnp.stack(grad_rows).reshape(3, 3, channels, channels).astype(jnp.bfloat16)
    padded_grad = jnp.pad(cotangent, ((0, 0), (1, 1), (1, 1)))
    grad_act = jnp.zeros((channels, height, width), jnp.float32)
    for row_off in range(3):
        for col_off in range(3):
            window = padded_grad[:, 2 - row_off:2 - row_off + height, 2 - col_off:2 - col_off + width]
            grad_act = grad_act + jnp.einsum("ohw,co->chw", window, conv_second[row_off, col_off].astype(jnp.float32))
    sigmoid_h = jax.nn.sigmoid(hidden_pre)
    grad_hidden = (grad_act * sigmoid_h * (1.0 + hidden_pre * (1.0 - sigmoid_h))).astype(jnp.bfloat16)
    return output, grad_weight, grad_hidden
```

```python
import jax
import jax.numpy as jnp
from jax import lax
from jax.experimental import pallas as pl
from jax.experimental.pallas import tpu as pltpu
from jax.sharding import PartitionSpec as P

MESH = pl.DeviceIdType.MESH
BF16 = jnp.bfloat16
F32 = jnp.float32

CH = 64
ROWS = 16
COLS = 256
CELLS = ROWS * COLS
LANES = CELLS + 2 * COLS
HALF = CELLS // 2
TILES = 16
CHANS = 8
CHIPS = 4
ALL = CH * CHANS
SHARD = 512
CAP = 64
PACK = 80
BLOCK = 1024
NT = (((1,), (1,)), ((), ()))

G, A, H = 0, 1, 2


def neighbour_sum(z):
    lanes = z.shape[1]
    col = lax.broadcasted_iota(jnp.int32, (CH, lanes), 1) % COLS
    left = jnp.where(col == 0, 0.0, pltpu.roll(z[:CH], 1, 1))
    right = jnp.where(col == COLS - 1, 0.0, pltpu.roll(z[2 * CH :], lanes - 1, 1))
    return z[CH : 2 * CH] + left + right


def kernel(
    grid_ref, gout_ref, feats_ref, owner_ref, valid_ref, cell_ref, w1_ref, w2_ref, b2_ref,
    out_ref, gw_ref, gh_ref,
    ga, aa, ha, zbuf, hidden_pre, g3, wb, wbt, packed, landed, masked, gw_out, gw_in,
    x_send, x_recv, e_send, e_recv, d_send, d_recv, s_send, s_recv, w_send, w_recv, g_send, g_recv,
):
    tile = lax.axis_index("tile")
    chan = lax.axis_index("chan")
    x, core = chan // 2, chan % 2
    bufs = (ga, aa, ha)
    chips = [x, (x + 3) % 4, (x + 1) % 4, (x + 2) % 4]
    right = (tile, ((x + 1) % 4) * 2 + core)
    left = (tile, ((x + 3) % 4) * 2 + core)
    sibling = (tile, x * 2 + (1 - core))
    has_up, has_down = tile > 0, tile < TILES - 1

    def rows_of(chip, which):
        return pl.ds(pl.multiple_of(chip * (2 * CH) + which * CH, CH), CH)

    def pair_of(chip):
        return pl.ds(pl.multiple_of(chip * (2 * CH), 2 * CH), 2 * CH)

    halves = (pl.ds(COLS, HALF), pl.ds(COLS + HALF, HALF))

    def remote(src, dst, send, recv, device):
        return pltpu.make_async_remote_copy(
            src_ref=src, dst_ref=dst, send_sem=send, recv_sem=recv, device_id=device, device_id_type=MESH
        )

    x_table = {
        0: (chips[0], 0, True, chips[1]),
        1: (chips[0], 1, True, chips[1]),
        2: (chips[1], 0, True, chips[3]),
        3: (chips[0], 0, False, chips[2]),
        4: (chips[0], 1, False, chips[2]),
        5: (chips[2], 1, False, chips[3]),
    }

    def x_copy(f, k, arriving=False):
        sent, half, to_right, received = x_table[k]
        place = bufs[f].at[rows_of(received if arriving else sent, core), halves[half]]
        return remote(place, place, x_send.at[f, k], x_recv.at[f, k], right if to_right else left)

    top, bottom = pl.ds(0, COLS), pl.ds(COLS + CELLS, COLS)
    first, last = pl.ds(COLS, COLS), pl.ds(CELLS, COLS)

    def e_copy(f, j, down):
        rows = rows_of(chips[j], core)
        k = 2 * j + down
        src = bufs[f].at[rows, last if down else first]
        dst = bufs[f].at[rows, top if down else bottom]
        device = (jnp.minimum(tile + 1, TILES - 1) if down else jnp.maximum(tile - 1, 0), chan)
        return remote(src, dst, e_send.at[f, k], e_recv.at[f, k], device)

    def e_start(f, j, down):
        @pl.when(has_down if down else has_up)
        def _():
            e_copy(f, j, down).start()

    def e_wait_recv(f, j):
        @pl.when(has_up)
        def _():
            e_copy(f, j, 1).wait_recv()

        @pl.when(has_down)
        def _():
            e_copy(f, j, 0).wait_recv()

    def d_copy(f, j, arriving=False):
        rows = rows_of(chips[j], 1 - core if arriving else core)
        place = bufs[f].at[rows, :]
        return remote(place, place, d_send.at[f, j], d_recv.at[f, j], sibling)

    def own_start(f, half):
        x_copy(f, 0 + half).start()
        x_copy(f, 3 + half).start()
        e_start(f, 0, half)

    def pass_on(f, j):
        e_wait_recv(f, j)
        d_copy(f, j).start()

    def near(f, forward):
        x_copy(f, 0, True).wait_recv()
        if forward:
            x_copy(f, 2).start()
        e_start(f, 1, 0)
        x_copy(f, 3, True).wait_recv()
        e_start(f, 2, 0)
        x_copy(f, 4, True).wait_recv()
        if forward:
            x_copy(f, 5).start()
        e_start(f, 2, 1)
        x_copy(f, 1, True).wait_recv()
        e_start(f, 1, 1)
        pass_on(f, 1)
        pass_on(f, 2)

    def far_arrive(f):
        x_copy(f, 2, True).wait_recv()
        e_start(f, 3, 0)
        x_copy(f, 5, True).wait_recv()
        e_start(f, 3, 1)

    def d_wait(f, j):
        d_copy(f, j, True).wait_recv()

    def products(buf, weights, pairs, block):
        total = None
        for r in range(3):
            lanes = pl.ds(pl.multiple_of(block * BLOCK + r * COLS, COLS), BLOCK)
            taps = pl.ds(r * 3 * CH, 3 * CH)
            if pairs is None:
                lhs, rhs = weights[taps, :], buf[:, lanes]
            else:
                lhs = [weights[taps, pair_of(p)] for p in pairs]
                rhs = [buf[pair_of(p), lanes] for p in pairs]
                lhs = lhs[0] if len(lhs) == 1 else jnp.concatenate(lhs, axis=1)
                rhs = rhs[0] if len(rhs) == 1 else jnp.concatenate(rhs, axis=0)
            term = jnp.dot(lhs, rhs, preferred_element_type=F32)
            total = term if total is None else total + term
        return total

    def conv_pass(buf, weights, pairs, start):
        @pl.loop(0, CELLS // BLOCK)
        def _(block):
            z = products(buf, weights, pairs, block)
            zbuf[block] = z if start else zbuf[block] + z

    def block_lanes(block):
        return pl.ds(pl.multiple_of(block * BLOCK, BLOCK), BLOCK)

    for buf in bufs:
        for chip in chips:
            @pl.when(tile == 0)
            def _(buf=buf, chip=chip):
                buf[rows_of(chip, core), top] = jnp.zeros((CH, COLS), BF16)

            @pl.when(tile == TILES - 1)
            def _(buf=buf, chip=chip):
                buf[rows_of(chip, core), bottom] = jnp.zeros((CH, COLS), BF16)

    ga[rows_of(x, core), pl.ds(COLS, CELLS)] = gout_ref[...]

    barrier = pltpu.get_barrier_semaphore()
    for step in range(1, TILES):
        pl.semaphore_signal(barrier, inc=1, device_id=((tile + step) % TILES, chan), device_id_type=MESH)
    for step in range(1, CHANS):
        pl.semaphore_signal(barrier, inc=1, device_id=(tile, (chan + step) % CHANS), device_id_type=MESH)
    pl.semaphore_wait(barrier, TILES + CHANS - 2)

    own_start(G, 0)
    own_start(G, 1)

    owners, usable = owner_ref[...], valid_ref[...] == 1
    tile_of = lax.broadcasted_iota(jnp.int32, (SHARD, 128), 1)
    named = jnp.where((owners == tile_of) & usable, 1.0, 0.0)
    lower = lax.broadcasted_iota(jnp.int32, (SHARD, SHARD), 0) >= lax.broadcasted_iota(jnp.int32, (SHARD, SHARD), 1)
    counts = jnp.dot(jnp.where(lower, 1.0, 0.0).astype(BF16), named.astype(BF16), preferred_element_type=F32)
    rank = jnp.sum(counts * named, axis=1, keepdims=True).astype(jnp.int32) - 1
    slot = jnp.where(usable, owners * 128 + (tile % 2) * CAP + rank, -1)
    cells = cell_ref[...]
    sub = lax.broadcasted_iota(jnp.int32, (PACK - CH, SHARD), 0)
    places = jnp.where(sub == 0, cells // COLS, jnp.where(sub == 1, cells % COLS, 0))
    rowed = jnp.concatenate([feats_ref[...], places.astype(F32).astype(BF16)], axis=0)
    for part in range(4):
        number = lax.broadcasted_iota(jnp.int32, (SHARD, 512), 1) + part * 512
        chosen = jnp.where(slot == number, 1.0, 0.0).astype(BF16)
        sent = jnp.dot(rowed, chosen, preferred_element_type=F32).astype(BF16)
        for k in range(4):
            packed[part * 4 + k] = sent[:, k * 128 : (k + 1) * 128]

    def s_copy(step, arriving=False):
        other = (tile + step) % TILES
        source = (tile + TILES - step) % TILES
        if arriving:
            place = landed.at[source]
            return remote(place, place, s_send.at[step], s_recv.at[step], (other, chan))
        return remote(packed.at[other], landed.at[tile], s_send.at[step], s_recv.at[step], (other, chan))

    for step in range(1, TILES):
        s_copy(step).start()
    landed[tile] = packed[tile]

    def w_copy(step, arriving=False):
        other = (chan + step) % CHANS
        source = (chan + CHANS - step) % CHANS
        if arriving:
            place = wb.at[source]
            return remote(place, place, w_send.at[step], w_recv.at[step], (tile, other))
        return remote(b2_ref.at[other], wb.at[chan], w_send.at[step], w_recv.at[step], (tile, other))

    for step in range(1, CHANS):
        w_copy(step).start()
    wb[chan] = b2_ref[chan]

    for step in range(1, TILES):
        s_copy(step, True).wait_recv()
    stations = jnp.concatenate([landed[2 * k] + landed[2 * k + 1] for k in range(TILES // 2)], axis=1)
    slots = stations.shape[1]
    station_row = stations[CH : CH + 1].astype(F32)
    station_col = stations[CH + 1 : CH + 2].astype(F32)
    spread = lax.broadcasted_iota(jnp.int32, (COLS, slots), 0).astype(F32)
    col_hot = jnp.where(station_col == spread, 1.0, 0.0).astype(BF16)
    for i in range(ROWS):
        keep = (station_row == float(i))
        masked[pl.ds(i * CH, CH), :] = jnp.where(keep, stations[:CH].astype(F32), 0.0).astype(BF16)
    for quarter in range(4):
        rows = pl.ds(quarter * 256, 256)
        sums = lax.dot_general(masked[rows, :], col_hot, NT, preferred_element_type=F32)
        for k in range(4):
            i = quarter * 4 + k
            cell = pl.ds(i * COLS, COLS)
            value = grid_ref[:, cell].astype(F32) + sums[k * CH : (k + 1) * CH]
            aa[rows_of(x, core), pl.ds((i + 1) * COLS, COLS)] = value.astype(BF16)
        if quarter == 1:
            own_start(A, 0)
    own_start(A, 1)

    pass_on(G, 0)
    g_col = lax.broadcasted_iota(jnp.int32, (CH, LANES), 1) % COLS
    own_g = ga[rows_of(x, core), :].astype(F32)
    g3[pl.ds(CH, CH), :] = ga[rows_of(x, core), :]
    g3[pl.ds(0, CH), :] = jnp.where(g_col == COLS - 1, 0.0, pltpu.roll(own_g, LANES - 1, 1)).astype(BF16)
    g3[pl.ds(2 * CH, CH), :] = jnp.where(g_col == 0, 0.0, pltpu.roll(own_g, 1, 1)).astype(BF16)

    pass_on(A, 0)
    for step in range(1, CHANS):
        w_copy(step, True).wait_recv()
    for s in range(CHANS // 2):
        two = jnp.concatenate([wb[2 * s], wb[2 * s + 1]], axis=0).astype(F32)
        wbt[:, pl.ds(s * 128, 128)] = two.T.astype(BF16)

    d_wait(A, 0)
    conv_pass(aa, w1_ref, [chips[0]], True)
    near(G, False)
    near(A, True)
    d_wait(A, 1)
    d_wait(A, 2)
    conv_pass(aa, w1_ref, [chips[1], chips[2]], False)
    far_arrive(A)
    x_copy(G, 2).start()
    x_copy(G, 5).start()
    pass_on(A, 3)
    d_wait(A, 3)
    for half in range(2):
        @pl.loop(2 * half, 2 * half + 2)
        def _(block):
            z = zbuf[block] + products(aa, w1_ref, [chips[3]], block)
            value = neighbour_sum(z)
            hidden_pre[:, block_lanes(block)] = value
            hidden = value * (1.0 / (1.0 + jnp.exp(-value)))
            lanes = pl.ds(pl.multiple_of(block * BLOCK + COLS, COLS), BLOCK)
            ha[rows_of(x, core), lanes] = hidden.astype(BF16)

        own_start(H, half)

    pass_on(H, 0)
    far_arrive(G)
    pass_on(G, 3)
    for j in range(4):
        d_wait(G, j)

    @pl.loop(0, CELLS // BLOCK)
    def _(block):
        grad_act = neighbour_sum(products(ga, wbt, None, block))
        value = hidden_pre[:, block_lanes(block)]
        s = 1.0 / (1.0 + jnp.exp(-value))
        gh_ref[:, block_lanes(block)] = (grad_act * s * (1.0 + value * (1.0 - s))).astype(BF16)

    def piece(step):
        return (tile + step) % TILES

    def g_copy(to):
        return remote(gw_out.at[to], gw_in.at[tile], g_send.at[to], g_recv.at[tile], (to, chan))

    def weight_terms(j):
        chip = chips[j]
        field = ha[pair_of(chip), pl.ds(COLS, CELLS)]
        for r in range(3):
            term = lax.dot_general(
                field, g3[:, pl.ds((2 - r) * COLS, CELLS)], NT, preferred_element_type=F32
            ).astype(BF16)
            for k in range(4):
                gw_out[chip * 4 + k, pl.ds(r * 32, 32), pl.ds(0, 3 * CH)] = term[k * 32 : (k + 1) * 32]
        for k in range(4):
            to = chip * 4 + k

            @pl.when(to != tile)
            def _(to=to):
                g_copy(to).start()

            @pl.when(to == tile)
            def _(to=to):
                gw_in[tile] = gw_out[to]

    d_wait(H, 0)
    conv_pass(ha, w2_ref, [chips[0]], True)
    weight_terms(0)
    near(H, True)
    d_wait(H, 1)
    d_wait(H, 2)
    conv_pass(ha, w2_ref, [chips[1], chips[2]], False)
    weight_terms(1)
    weight_terms(2)
    far_arrive(H)
    pass_on(H, 3)
    d_wait(H, 3)
    weight_terms(3)

    @pl.loop(0, CELLS // BLOCK)
    def _(block):
        z = zbuf[block] + products(ha, w2_ref, [chips[3]], block)
        lanes = pl.ds(pl.multiple_of(block * BLOCK + COLS, COLS), BLOCK)
        branch = neighbour_sum(z)
        out_ref[:, block_lanes(block)] = (aa[rows_of(x, core), lanes].astype(F32) + branch).astype(BF16)

    for step in range(1, TILES):
        source = piece(step)
        place = gw_in.at[source]
        remote(place, place, g_send.at[source], g_recv.at[source], (source, chan)).wait_recv()
    total = gw_in[0].astype(F32)
    for k in range(1, TILES):
        total = total + gw_in[k].astype(F32)
    gw_ref[...] = total.astype(BF16)

    for f in (G, A, H):
        for k in range(6):
            x_copy(f, k).wait_send()
        for j in range(4):
            d_copy(f, j).wait_send()

            @pl.when(has_up)
            def _(f=f, j=j):
                e_copy(f, j, 0).wait_send()

            @pl.when(has_down)
            def _(f=f, j=j):
                e_copy(f, j, 1).wait_send()

    for step in range(1, TILES):
        s_copy(step).wait_send()
        g_copy(piece(step)).wait_send()
    for step in range(1, CHANS):
        w_copy(step).wait_send()


def local(grid, station_feats, owner_tile, station_cell, valid, conv_first, conv_second, grad_out):
    w1 = conv_first.transpose(0, 1, 3, 2).reshape(9 * CH, ALL)
    w2 = conv_second.transpose(0, 1, 3, 2).reshape(9 * CH, ALL)
    back = conv_second[::-1, ::-1].reshape(9, CHANS, CH, CH).transpose(1, 3, 0, 2).reshape(CHANS, CH, 9 * CH)
    back = jnp.pad(back, ((0, 0), (0, 0), (0, CH)))
    vmem = pl.BlockSpec(memory_space=pltpu.VMEM)
    dma = pltpu.SemaphoreType.DMA
    output, grad_weight, grad_hidden = pl.pallas_call(
        kernel,
        out_shape=(
            jax.ShapeDtypeStruct((CH, CELLS), BF16),
            jax.ShapeDtypeStruct((96, 256), BF16),
            jax.ShapeDtypeStruct((CH, CELLS), BF16),
        ),
        in_specs=[vmem] * 9,
        out_specs=(vmem,) * 3,
        scratch_shapes=[
            pltpu.VMEM((ALL, LANES), BF16),
            pltpu.VMEM((ALL, LANES), BF16),
            pltpu.VMEM((ALL, LANES), BF16),
            pltpu.VMEM((CELLS // BLOCK, 3 * CH, BLOCK), F32),
            pltpu.VMEM((CH, CELLS), F32),
            pltpu.VMEM((3 * CH, LANES), BF16),
            pltpu.VMEM((CHANS, CH, 10 * CH), BF16),
            pltpu.VMEM((10 * CH, ALL), BF16),
            pltpu.VMEM((TILES, PACK, 128), BF16),
            pltpu.VMEM((TILES, PACK, 128), BF16),
            pltpu.VMEM((ROWS * CH, TILES * CAP), BF16),
            pltpu.VMEM((TILES, 96, 256), BF16),
            pltpu.VMEM((TILES, 96, 256), BF16),
            dma((3, 6)), dma((3, 6)), dma((3, 8)), dma((3, 8)), dma((3, 4)), dma((3, 4)),
            dma((TILES,)), dma((TILES,)), dma((CHANS,)), dma((CHANS,)), dma((TILES,)), dma((TILES,)),
        ],
        compiler_params=pltpu.CompilerParams(
            collective_id=0, has_side_effects=True, vmem_limit_bytes=56 * 1024 * 1024
        ),
    )(
        grid.reshape(CH, CELLS),
        grad_out.reshape(CH, CELLS),
        station_feats,
        owner_tile,
        valid.reshape(SHARD, 1),
        station_cell.reshape(1, SHARD),
        w1,
        w2,
        back,
    )
    grad_weight = grad_weight[:, : 3 * CH].reshape(3, 32, 3, CH).transpose(0, 2, 1, 3)
    return (output.reshape(CH, ROWS, COLS), grad_weight, grad_hidden.reshape(CH, ROWS, COLS))


def solution(mesh):
    return jax.shard_map(
        local,
        mesh=mesh,
        in_specs=(
            P("chan", "tile", None),
            P("chan", "tile"),
            P("tile", None),
            P("tile"),
            P("tile"),
            P(None, None, None, "chan"),
            P(None, None, None, "chan"),
            P("chan", "tile", None),
        ),
        out_specs=(P("chan", "tile", None), P(None, None, "tile", "chan"), P("chan", "tile", None)),
        check_vma=False,
    )
```

```python
import jax
import jax.numpy as jnp
from jax import lax
from jax.experimental import pallas as pl
from jax.experimental.pallas import tpu as pltpu
from jax.sharding import PartitionSpec as P

MESH = pl.DeviceIdType.MESH
BF16 = jnp.bfloat16
F32 = jnp.float32

CH = 64
ROWS = 16
COLS = 256
CELLS = ROWS * COLS
LANES = CELLS + 2 * COLS
BLOCK = CELLS // 2
TILES = 16
CHANS = 8
ALL = CH * CHANS
SHARD = 512
CAP = 64
PACK = 80
PART = 32
NT = (((1,), (1,)), ((), ()))

G, A, H = 0, 1, 2


def shifted(values, by):
    lanes = values.shape[1]
    col = lax.broadcasted_iota(jnp.int32, values.shape, 1) % COLS
    if by == 1:
        return jnp.where(col == 0, 0.0, pltpu.roll(values, 1, 1))
    return jnp.where(col == COLS - 1, 0.0, pltpu.roll(values, lanes - 1, 1))


def neighbour_sum(z):
    return z[CH : 2 * CH] + shifted(z[:CH], 1) + shifted(z[2 * CH :], -1)


def kernel(
    grid_ref, gout_ref, feats_ref, marks_ref, w1_ref, w2_ref,
    out_ref, gw_ref, gh_ref,
    ga, aa, ha, zbuf, hidden_pre, h3, b2, wb, wbt, packed, landed, masked,
    gw_out, gw_one, gw_mid, gw_two, gw_fin, gw_land,
    x_send, x_recv, e_send, e_recv, d_send, d_recv, s_send, s_recv, w_send, w_recv, v_send, v_recv,
    one_send, one_recv, two_send, two_recv, three_send, three_recv,
):
    tile = lax.axis_index("tile")
    chan = lax.axis_index("chan")
    x, core = chan // 2, chan % 2
    y, z = tile // 4, tile % 4
    bufs = (ga, aa, ha)
    chips = [x, (x + 3) % 4, (x + 1) % 4, (x + 2) % 4]
    right = (tile, chips[2] * 2 + core)
    left = (tile, chips[1] * 2 + core)
    sibling = (tile, x * 2 + (1 - core))
    has_up, has_down = tile > 0, tile < TILES - 1

    barrier = pltpu.get_barrier_semaphore()
    for step in range(1, TILES):
        pl.semaphore_signal(barrier, inc=1, device_id=((tile + step) % TILES, chan), device_id_type=MESH)
    for step in range(1, CHANS):
        pl.semaphore_signal(barrier, inc=1, device_id=(tile, (chan + step) % CHANS), device_id_type=MESH)

    def rows_of(chip, which, low=0, size=CH):
        return pl.ds(pl.multiple_of(chip * (2 * CH) + which * CH + low, size), size)

    def pair_of(chip):
        return pl.ds(pl.multiple_of(chip * (2 * CH), 2 * CH), 2 * CH)

    own = rows_of(x, core)
    halves = (pl.ds(COLS, BLOCK), pl.ds(COLS + BLOCK, BLOCK))
    quarters = [pl.ds(COLS + q * 1024, 1024) for q in range(4)]
    top, bottom = pl.ds(0, COLS), pl.ds(COLS + CELLS, COLS)
    first, last = pl.ds(COLS, COLS), pl.ds(CELLS, COLS)
    inner = pl.ds(COLS, CELLS)

    def remote(src, dst, send, recv, device):
        return pltpu.make_async_remote_copy(
            src_ref=src, dst_ref=dst, send_sem=send, recv_sem=recv, device_id=device, device_id_type=MESH
        )

    x_table = (
        (0, halves[0], 0, CH, True, 1),
        (0, halves[1], 0, CH, True, 1),
        (0, halves[0], 0, CH, False, 2),
        (0, halves[1], 0, CH, False, 2),
        (1, halves[0], 0, CH // 2, True, 3),
        (1, quarters[3], 0, CH // 2, True, 3),
        (1, quarters[2], 0, CH // 2, True, 3),
        (2, halves[0], CH // 2, CH // 2, False, 3),
        (2, quarters[3], CH // 2, CH // 2, False, 3),
        (2, quarters[2], CH // 2, CH // 2, False, 3),
    )

    def x_copy(f, k, arriving=False):
        sent, lanes, low, size, to_right, received = x_table[k]
        place = bufs[f].at[rows_of(chips[received if arriving else sent], core, low, size), lanes]
        return remote(place, place, x_send.at[f, k], x_recv.at[f, k], right if to_right else left)

    def e_copy(f, j, down, arriving=False):
        rows = rows_of(chips[j], core)
        k = 2 * j + down
        src = bufs[f].at[rows, last if down else first]
        dst = bufs[f].at[rows, top if down else bottom]
        device = (jnp.minimum(tile + 1, TILES - 1) if down else jnp.maximum(tile - 1, 0), chan)
        return remote(dst if arriving else src, dst, e_send.at[f, k], e_recv.at[f, k], device)

    def e_start(f, j, down):
        @pl.when(has_down if down else has_up)
        def _():
            e_copy(f, j, down).start()

    def e_wait_recv(f, j, down):
        @pl.when(has_up if down else has_down)
        def _():
            e_copy(f, j, down, True).wait_recv()

    d_table = (
        (0, pl.ds(0, LANES)),
        (1, pl.ds(0, LANES)),
        (2, pl.ds(0, LANES)),
        (3, halves[0]),
        (3, quarters[3]),
        (3, quarters[2]),
        (3, top),
        (3, bottom),
    )

    def d_copy(f, k, arriving=False):
        j, lanes = d_table[k]
        place = bufs[f].at[rows_of(chips[j], 1 - core if arriving else core), lanes]
        return remote(place, place, d_send.at[f, k], d_recv.at[f, k], sibling)

    def own_start(f, half):
        x_copy(f, half).start()
        x_copy(f, 2 + half).start()
        e_start(f, 0, half)

    def pass_on(f, j):
        e_wait_recv(f, j, 1)
        e_wait_recv(f, j, 0)
        d_copy(f, j).start()

    def forward(f, ks):
        for k in ks:
            x_copy(f, k).start()

    def near(f, onward):
        x_copy(f, 0, True).wait_recv()
        if onward:
            forward(f, (4,))
        e_start(f, 1, 0)
        x_copy(f, 2, True).wait_recv()
        if onward:
            forward(f, (7,))
        e_start(f, 2, 0)
        x_copy(f, 1, True).wait_recv()
        if onward:
            forward(f, (5, 6))
        e_start(f, 1, 1)
        x_copy(f, 3, True).wait_recv()
        if onward:
            forward(f, (8, 9))
        e_start(f, 2, 1)

    def far(f):
        x_copy(f, 4, True).wait_recv()
        x_copy(f, 7, True).wait_recv()
        e_start(f, 3, 0)
        d_copy(f, 3).start()
        x_copy(f, 5, True).wait_recv()
        x_copy(f, 8, True).wait_recv()
        e_start(f, 3, 1)
        d_copy(f, 4).start()
        x_copy(f, 6, True).wait_recv()
        x_copy(f, 9, True).wait_recv()
        d_copy(f, 5).start()

    def far_edges(f):
        e_wait_recv(f, 3, 1)
        d_copy(f, 6).start()
        e_wait_recv(f, 3, 0)
        d_copy(f, 7).start()

    def d_wait(f, j):
        for k in range(len(d_table)):
            if d_table[k][0] == j:
                d_copy(f, k, True).wait_recv()

    def products(buf, weights, pairs, block):
        total = None
        for r in range(3):
            lanes = pl.ds(pl.multiple_of(block * BLOCK + r * COLS, COLS), BLOCK)
            taps = pl.ds(r * 3 * CH, 3 * CH)
            if pairs is None:
                lhs, rhs = weights[taps, :], buf[:, lanes]
            else:
                lhs = [weights[taps, pair_of(p)] for p in pairs]
                rhs = [buf[pair_of(p), lanes] for p in pairs]
                lhs = lhs[0] if len(lhs) == 1 else jnp.concatenate(lhs, axis=1)
                rhs = rhs[0] if len(rhs) == 1 else jnp.concatenate(rhs, axis=0)
            term = jnp.dot(lhs, rhs, preferred_element_type=F32)
            total = term if total is None else total + term
        return total

    def conv_pass(buf, weights, pairs, start):
        @pl.loop(0, 2)
        def _(block):
            terms = products(buf, weights, pairs, block)
            zbuf[block] = terms if start else zbuf[block] + terms

    def block_lanes(block, skip=0):
        return pl.ds(pl.multiple_of(block * BLOCK + skip, COLS), BLOCK)

    def block_rows(block):
        return pl.ds(pl.multiple_of(block * (ROWS // 2), ROWS // 2), ROWS // 2)

    with jax.named_scope("prepare"):
        ga[own, inner] = gout_ref[...].reshape(CH, CELLS)
        for buf in bufs:
            for chip in chips:
                @pl.when(tile == 0)
                def _(buf=buf, chip=chip):
                    buf[rows_of(chip, core), top] = jnp.zeros((CH, COLS), BF16)

                @pl.when(tile == TILES - 1)
                def _(buf=buf, chip=chip):
                    buf[rows_of(chip, core), bottom] = jnp.zeros((CH, COLS), BF16)

        marks = marks_ref[...]
        columns = marks.astype(F32).T
        owners, usable = columns[:, 0:1].astype(jnp.int32), columns[:, 1:2] == 1.0
        tile_of = lax.broadcasted_iota(jnp.int32, (SHARD, 128), 1)
        named = jnp.where((owners == tile_of) & usable, 1.0, 0.0)
        lower = lax.broadcasted_iota(jnp.int32, (SHARD, SHARD), 0) >= lax.broadcasted_iota(jnp.int32, (SHARD, SHARD), 1)
        counts = jnp.dot(jnp.where(lower, 1.0, 0.0).astype(BF16), named.astype(BF16), preferred_element_type=F32)
        rank = jnp.sum(counts * named, axis=1, keepdims=True).astype(jnp.int32) - 1
        slot = jnp.where(usable, owners * 128 + (tile % 2) * CAP + rank, -1)
        cells = marks[2:3]
        sub = lax.broadcasted_iota(jnp.int32, (PACK - CH, SHARD), 0)
        places = jnp.where(sub == 0, cells // COLS, jnp.where(sub == 1, cells % COLS, 0))
        rowed = jnp.concatenate([feats_ref[...], places.astype(F32).astype(BF16)], axis=0)
        for part in range(4):
            number = lax.broadcasted_iota(jnp.int32, (SHARD, 512), 1) + part * 512
            chosen = jnp.where(slot == number, 1.0, 0.0).astype(BF16)
            sent = jnp.dot(rowed, chosen, preferred_element_type=F32).astype(BF16)
            for k in range(4):
                packed[part * 4 + k] = sent[:, k * 128 : (k + 1) * 128]
        landed[tile] = packed[tile]

    with jax.named_scope("barrier_wait"):
        pl.semaphore_wait(barrier, TILES + CHANS - 2)

    def s_copy(step, arriving=False):
        other = (tile + step) % TILES
        place = landed.at[(tile + TILES - step) % TILES]
        if arriving:
            return remote(place, place, s_send.at[step], s_recv.at[step], (other, chan))
        return remote(packed.at[other], landed.at[tile], s_send.at[step], s_recv.at[step], (other, chan))

    def w_copy(step, arriving=False):
        other = (chan + step) % CHANS
        rows = pl.ds(pl.multiple_of(z * 16, 16), 16)
        place = wb.at[(chan + CHANS - step) % CHANS, rows]
        if arriving:
            return remote(place, place, w_send.at[step], w_recv.at[step], (tile, other))
        return remote(b2.at[other, rows], wb.at[chan, rows], w_send.at[step], w_recv.at[step], (tile, other))

    def v_copy(step, arriving=False):
        other = y * 4 + (z + step) % 4
        quarter = (z + 4 - step) % 4 if arriving else z
        place = wb.at[:, pl.ds(pl.multiple_of(quarter * 16, 16), 16)]
        return remote(place, place, v_send.at[step], v_recv.at[step], (other, chan))

    with jax.named_scope("first_sends"):
        for step in range(1, TILES):
            s_copy(step).start()
        own_start(G, 0)
        own_start(G, 1)

    with jax.named_scope("weight_pieces"):
        lane = lax.broadcasted_iota(jnp.int32, (CH, 128), 1)
        for chip in range(4):
            taps = [w2_ref[pl.ds((8 - n) * CH, CH), pl.ds(chip * 128, 128)].astype(F32) for n in range(9)]
            turned = [pltpu.roll(tap, CH, 1) for tap in taps]
            for k in range(5):
                n = 2 * k
                even = jnp.where(lane < CH, taps[n], turned[n + 1] if n < 8 else 0.0)
                odd = jnp.where(lane < CH, turned[n], taps[n + 1] if n < 8 else 0.0)
                b2[2 * chip, :, pl.ds(k * 128, 128)] = even.astype(BF16)
                b2[2 * chip + 1, :, pl.ds(k * 128, 128)] = odd.astype(BF16)
        for step in range(1, CHANS):
            w_copy(step).start()
        mine = pl.ds(pl.multiple_of(z * 16, 16), 16)
        wb[chan, mine] = b2[chan, mine]

    with jax.named_scope("station_wait"):
        for step in range(1, TILES):
            s_copy(step, True).wait_recv()
    with jax.named_scope("assimilate"):
        stations = jnp.concatenate([landed[2 * k] + landed[2 * k + 1] for k in range(TILES // 2)], axis=1)
        slots = stations.shape[1]
        station_row = stations[CH : CH + 1].astype(F32)
        station_col = stations[CH + 1 : CH + 2].astype(F32)
        spread = lax.broadcasted_iota(jnp.int32, (COLS, slots), 0).astype(F32)
        col_hot = jnp.where(station_col == spread, 1.0, 0.0).astype(BF16)
        features = stations[:CH].astype(F32)
        for i in range(ROWS):
            masked[pl.ds(i * CH, CH), :] = jnp.where(station_row == float(i), features, 0.0).astype(BF16)
        background = grid_ref[...].reshape(CH, CELLS)
        for half in range(2):
            rows = pl.ds(half * 512, 512)
            sums = lax.dot_general(masked[rows, :], col_hot, NT, preferred_element_type=F32)
            for k in range(8):
                i = half * 8 + k
                value = background[:, i * COLS : (i + 1) * COLS].astype(F32) + sums[k * CH : (k + 1) * CH]
                aa[own, pl.ds((i + 1) * COLS, COLS)] = value.astype(BF16)
            own_start(A, half)

    with jax.named_scope("pass_on_0"):
        pass_on(G, 0)
        for step in range(1, CHANS):
            w_copy(step, True).wait_recv()
        for step in range(1, 4):
            v_copy(step).start()
        pass_on(A, 0)
    with jax.named_scope("wait_A0"):
        d_wait(A, 0)
    with jax.named_scope("conv1_pass1"):
        conv_pass(aa, w1_ref, [chips[0]], True)
    with jax.named_scope("near_G"):
        near(G, False)
        pass_on(G, 1)
        pass_on(G, 2)
    with jax.named_scope("turn_weights"):
        for step in range(1, 4):
            v_copy(step, True).wait_recv()
        for s in range(CHANS // 2):
            two = jnp.concatenate([wb[2 * s], wb[2 * s + 1]], axis=0).astype(F32)
            wbt[:, pl.ds(s * 128, 128)] = two.T.astype(BF16)
    with jax.named_scope("near_A"):
        near(A, True)
        pass_on(A, 1)
        pass_on(A, 2)
    with jax.named_scope("wait_A12"):
        d_wait(A, 1)
        d_wait(A, 2)
    with jax.named_scope("conv1_pass2"):
        conv_pass(aa, w1_ref, [chips[1], chips[2]], False)
    with jax.named_scope("far_A"):
        far(A)
        forward(G, (4, 7, 5, 8, 6, 9))
        far_edges(A)
    with jax.named_scope("wait_A3"):
        d_wait(A, 3)
    with jax.named_scope("conv1_pass3"):
        for half in range(2):
            value = neighbour_sum(zbuf[half] + products(aa, w1_ref, [chips[3]], half))
            hidden_pre[:, block_lanes(half)] = value
            hidden = value * (1.0 / (1.0 + jnp.exp(-value)))
            ha[own, block_lanes(half, COLS)] = hidden.astype(BF16)
            own_start(H, half)

    def weight_terms(group):
        for r in range(3):
            lanes = pl.ds((2 - r) * COLS, CELLS)
            against = jnp.concatenate([ga[pair_of(chips[2 * group + k]), lanes] for k in range(2)], axis=0)
            term = lax.dot_general(h3[...], against, NT, preferred_element_type=F32).astype(BF16)
            for part in range(2):
                gw_out[part, r, :, pl.ds(group * 256, 256)] = term[part * 96 : (part + 1) * 96]

    group_lanes = (pl.ds(0, 256), pl.ds(256, 256))
    collects = z // 2 == core
    owns = collects & (y == x)

    def one_copy(part, group):
        target = 2 * core + part
        slot = jnp.maximum((target + 4 - z) % 4 - 1, 0)
        return remote(
            gw_out.at[part, :, :, group_lanes[group]],
            gw_one.at[slot, :, :, group_lanes[group]],
            one_send.at[part, group],
            one_recv.at[slot, group],
            (y * 4 + target, chan),
        )

    def one_start(group):
        for part in range(2):
            @pl.when(2 * core + part != z)
            def _(part=part):
                one_copy(part, group).start()

    def two_copy(group):
        slot = jnp.maximum((x + 4 - y) % 4 - 1, 0)
        return remote(
            gw_mid.at[:, :, group_lanes[group]],
            gw_two.at[slot, :, :, group_lanes[group]],
            two_send.at[group],
            two_recv.at[slot, group],
            (x * 4 + z, chan),
        )

    def slot_wait(buf, recv, slot, group):
        place = buf.at[slot, :, :, group_lanes[group]]
        remote(place, place, recv.at[slot, group], recv.at[slot, group], (tile, chan)).wait_recv()

    def collect(group):
        @pl.when(collects)
        def _():
            for slot in range(3):
                slot_wait(gw_one, one_recv, slot, group)
            lanes = group_lanes[group]
            total = gw_out[z % 2, :, :, lanes].astype(F32)
            for slot in range(3):
                total = total + gw_one[slot, :, :, lanes].astype(F32)
            gw_mid[:, :, lanes] = total.astype(BF16)

            @pl.when(y != x)
            def _():
                two_copy(group).start()

    def finish(group):
        @pl.when(owns)
        def _():
            for slot in range(3):
                slot_wait(gw_two, two_recv, slot, group)
            lanes = group_lanes[group]
            total = gw_mid[:, :, lanes].astype(F32)
            for slot in range(3):
                total = total + gw_two[slot, :, :, lanes].astype(F32)
            gw_fin[:, :, lanes] = total.astype(BF16)
            for k in range(2):
                j = 2 * group + k
                for which in range(2):
                    if j == 0:
                        @pl.when(core != which)
                        def _(j=j, which=which):
                            three_copy(j, which).start()
                    else:
                        three_copy(j, which).start()
            if group == 0:
                gw_land[...] = gw_fin[:, :, pl.ds(0, 128)]

    def three_copy(j, which):
        return remote(
            gw_fin.at[:, :, pl.ds(j * 128, 128)],
            gw_land,
            three_send.at[j, which],
            three_recv.at[0],
            (tile, chips[j] * 2 + which),
        )

    with jax.named_scope("hidden_columns"):
        mine_h = ha[own, inner].astype(F32)
        moved = (shifted(mine_h, 1), mine_h, shifted(mine_h, -1))
        for part in range(2):
            for q in range(3):
                h3[pl.ds(part * 96 + q * PART, PART), :] = moved[q][part * PART : (part + 1) * PART].astype(BF16)
    with jax.named_scope("weight_terms_0"):
        d_wait(G, 0)
        d_wait(G, 1)
        d_wait(G, 2)
        weight_terms(0)
        one_start(0)
    with jax.named_scope("pass_on_H0"):
        pass_on(H, 0)
    with jax.named_scope("far_G"):
        far(G)
        far_edges(G)
        d_wait(G, 3)
    with jax.named_scope("weight_terms_1"):
        weight_terms(1)
        one_start(1)
    with jax.named_scope("grad_hidden"):
        @pl.loop(0, 2)
        def _(block):
            grad_act = neighbour_sum(products(ga, wbt, None, block))
            value = hidden_pre[:, block_lanes(block)]
            s = 1.0 / (1.0 + jnp.exp(-value))
            result = (grad_act * s * (1.0 + value * (1.0 - s))).astype(BF16)
            gh_ref[:, block_rows(block), :] = result.reshape(CH, ROWS // 2, COLS)
    with jax.named_scope("near_H"):
        near(H, True)
        pass_on(H, 1)
        pass_on(H, 2)
    with jax.named_scope("collect_0"):
        collect(0)
    with jax.named_scope("conv2_pass1"):
        d_wait(H, 0)
        conv_pass(ha, w2_ref, [chips[0]], True)
    with jax.named_scope("collect_1"):
        collect(1)
    with jax.named_scope("conv2_pass2"):
        d_wait(H, 1)
        d_wait(H, 2)
        conv_pass(ha, w2_ref, [chips[1], chips[2]], False)
    with jax.named_scope("far_H"):
        far(H)
        far_edges(H)
    with jax.named_scope("finish"):
        finish(0)
        finish(1)
    with jax.named_scope("wait_H3"):
        d_wait(H, 3)
    with jax.named_scope("conv2_pass3"):
        for half in range(2):
            branch = neighbour_sum(zbuf[half] + products(ha, w2_ref, [chips[3]], half))
            result = (aa[own, block_lanes(half, COLS)].astype(F32) + branch).astype(BF16)
            out_ref[:, half * (ROWS // 2) : (half + 1) * (ROWS // 2), :] = result.reshape(CH, ROWS // 2, COLS)
    with jax.named_scope("grad_weight"):
        @pl.when(jnp.logical_not(owns))
        def _():
            remote(gw_land, gw_land, three_recv.at[0], three_recv.at[0], (tile, chan)).wait_recv()

        for r in range(3):
            piece = gw_land[r].astype(F32)
            piece = jnp.where(core == 0, piece, pltpu.roll(piece, CH, 1))[:, :CH].astype(BF16)
            for q in range(3):
                gw_ref[r, q] = piece[q * PART : (q + 1) * PART]

    with jax.named_scope("sends_done"):
        for f in (G, A, H):
            for k in range(len(x_table)):
                x_copy(f, k).wait_send()
            for k in range(len(d_table)):
                d_copy(f, k).wait_send()
            for j in range(4):
                @pl.when(has_up)
                def _(f=f, j=j):
                    e_copy(f, j, 0).wait_send()

                @pl.when(has_down)
                def _(f=f, j=j):
                    e_copy(f, j, 1).wait_send()

        for step in range(1, TILES):
            s_copy(step).wait_send()
        for step in range(1, CHANS):
            w_copy(step).wait_send()
        for step in range(1, 4):
            v_copy(step).wait_send()
        for group in range(2):
            for part in range(2):
                @pl.when(2 * core + part != z)
                def _(part=part, group=group):
                    one_copy(part, group).wait_send()

            @pl.when(collects & (y != x))
            def _(group=group):
                two_copy(group).wait_send()

        @pl.when(owns)
        def _():
            for j in range(4):
                for which in range(2):
                    if j == 0:
                        @pl.when(core != which)
                        def _(j=j, which=which):
                            three_copy(j, which).wait_send()
                    else:
                        three_copy(j, which).wait_send()


def local(grid, station_feats, owner_tile, station_cell, valid, conv_first, conv_second, grad_out):
    w1 = conv_first.transpose(0, 1, 3, 2).reshape(9 * CH, ALL)
    w2 = conv_second.transpose(0, 1, 3, 2).reshape(9 * CH, ALL)
    marks = jnp.concatenate(
        [owner_tile.reshape(1, SHARD), valid.reshape(1, SHARD), station_cell.reshape(1, SHARD), jnp.zeros((5, SHARD), jnp.int32)]
    )
    vmem = pl.BlockSpec(memory_space=pltpu.VMEM)
    dma = pltpu.SemaphoreType.DMA
    return pl.pallas_call(
        kernel,
        out_shape=(
            jax.ShapeDtypeStruct((CH, ROWS, COLS), BF16),
            jax.ShapeDtypeStruct((3, 3, PART, CH), BF16),
            jax.ShapeDtypeStruct((CH, ROWS, COLS), BF16),
        ),
        in_specs=[vmem] * 6,
        out_specs=(vmem,) * 3,
        scratch_shapes=[
            pltpu.VMEM((ALL, LANES), BF16),
            pltpu.VMEM((ALL, LANES), BF16),
            pltpu.VMEM((ALL, LANES), BF16),
            pltpu.VMEM((2, 3 * CH, BLOCK), F32),
            pltpu.VMEM((CH, CELLS), F32),
            pltpu.VMEM((3 * CH, CELLS), BF16),
            pltpu.VMEM((CHANS, CH, 10 * CH), BF16),
            pltpu.VMEM((CHANS, CH, 10 * CH), BF16),
            pltpu.VMEM((10 * CH, ALL), BF16),
            pltpu.VMEM((TILES, PACK, 128), BF16),
            pltpu.VMEM((TILES, PACK, 128), BF16),
            pltpu.VMEM((ROWS * CH, TILES * CAP), BF16),
            pltpu.VMEM((2, 3, 96, ALL), BF16),
            pltpu.VMEM((3, 3, 96, ALL), BF16),
            pltpu.VMEM((3, 96, ALL), BF16),
            pltpu.VMEM((3, 3, 96, ALL), BF16),
            pltpu.VMEM((3, 96, ALL), BF16),
            pltpu.VMEM((3, 96, 128), BF16),
            dma((3, 10)), dma((3, 10)), dma((3, 8)), dma((3, 8)), dma((3, 8)), dma((3, 8)),
            dma((TILES,)), dma((TILES,)), dma((CHANS,)), dma((CHANS,)), dma((4,)), dma((4,)),
            dma((2, 2)), dma((3, 2)), dma((2,)), dma((3, 2)), dma((4, 2)), dma((1,)),
        ],
        compiler_params=pltpu.CompilerParams(
            collective_id=0, has_side_effects=True, vmem_limit_bytes=56 * 1024 * 1024
        ),
    )(grid, grad_out, station_feats, marks, w1, w2)


def solution(mesh):
    return jax.shard_map(
        local,
        mesh=mesh,
        in_specs=(
            P("chan", "tile", None),
            P("chan", "tile"),
            P("tile", None),
            P("tile"),
            P("tile"),
            P(None, None, None, "chan"),
            P(None, None, None, "chan"),
            P("chan", "tile", None),
        ),
        out_specs=(P("chan", "tile", None), P(None, None, "tile", "chan"), P("chan", "tile", None)),
        check_vma=False,
    )
```

```python
import jax
import jax.numpy as jnp
from jax import lax
from jax.experimental import pallas as pl
from jax.experimental.pallas import tpu as pltpu
from jax.sharding import PartitionSpec as P

MESH = pl.DeviceIdType.MESH
BF16 = jnp.bfloat16
F32 = jnp.float32

CH = 64
ROWS = 16
COLS = 256
CELLS = ROWS * COLS
LANES = CELLS + 2 * COLS
BLOCK = CELLS // 2
TILES = 16
CHANS = 8
ALL = CH * CHANS
SHARD = 512
CAP = 64
PACK = 96
PART = 32
NT = (((1,), (1,)), ((), ()))

G, A, H = 0, 1, 2


def shifted(values, by):
    lanes = values.shape[1]
    col = lax.broadcasted_iota(jnp.int32, values.shape, 1) % COLS
    if by == 1:
        return jnp.where(col == 0, 0.0, pltpu.roll(values, 1, 1))
    return jnp.where(col == COLS - 1, 0.0, pltpu.roll(values, lanes - 1, 1))


def neighbour_sum(z):
    return z[CH : 2 * CH] + shifted(z[:CH], 1) + shifted(z[2 * CH :], -1)


def kernel(
    feats_ref, owner_ref, valid_ref, cell_ref, gout_hbm, grid_hbm, w1_hbm, w2_hbm,
    out_ref, gw_ref, gh_ref,
    gout_ref, grid_ref, w1_ref, w2_ref, in_sem, ga, aa, ha, zbuf, hidden_pre, h3, b2, wb, wbt, packed, landed, masked,
    gw_out, gw_one, gw_mid, gw_two, gw_fin, gw_land,
    x_send, x_recv, e_send, e_recv, d_send, d_recv, s_send, s_recv, w_send, w_recv, v_send, v_recv,
    one_send, one_recv, two_send, two_recv, three_send, three_recv,
):
    tile = lax.axis_index("tile")
    chan = lax.axis_index("chan")
    x, core = chan // 2, chan % 2
    y, z = tile // 4, tile % 4
    bufs = (ga, aa, ha)
    chips = [x, (x + 3) % 4, (x + 1) % 4, (x + 2) % 4]
    right = (tile, chips[2] * 2 + core)
    left = (tile, chips[1] * 2 + core)
    sibling = (tile, x * 2 + (1 - core))
    has_up, has_down = tile > 0, tile < TILES - 1

    inward = [
        pltpu.make_async_copy(src, dst, in_sem.at[k])
        for k, (src, dst) in enumerate(
            ((gout_hbm, gout_ref), (w2_hbm, w2_ref), (grid_hbm, grid_ref), (w1_hbm, w1_ref))
        )
    ]
    for copy in inward:
        copy.start()

    barrier = pltpu.get_barrier_semaphore()
    for step in range(1, TILES):
        pl.semaphore_signal(barrier, inc=1, device_id=((tile + step) % TILES, chan), device_id_type=MESH)
    for step in range(1, CHANS):
        pl.semaphore_signal(barrier, inc=1, device_id=(tile, (chan + step) % CHANS), device_id_type=MESH)

    def rows_of(chip, which, low=0, size=CH):
        return pl.ds(pl.multiple_of(chip * (2 * CH) + which * CH + low, size), size)

    def pair_of(chip):
        return pl.ds(pl.multiple_of(chip * (2 * CH), 2 * CH), 2 * CH)

    own = rows_of(x, core)
    quarters = [pl.ds(COLS + q * 1024, 1024) for q in range(4)]
    middle = pl.ds(COLS + 1024, BLOCK)
    top, bottom = pl.ds(0, COLS), pl.ds(COLS + CELLS, COLS)
    first, last = pl.ds(COLS, COLS), pl.ds(CELLS, COLS)
    inner = pl.ds(COLS, CELLS)

    def remote(src, dst, send, recv, device):
        return pltpu.make_async_remote_copy(
            src_ref=src, dst_ref=dst, send_sem=send, recv_sem=recv, device_id=device, device_id_type=MESH
        )

    outer = (quarters[0], quarters[3], middle)
    x_table = (
        *((0, lanes, 0, CH, True, 1) for lanes in outer),
        *((0, lanes, 0, CH, False, 2) for lanes in outer),
        *((1, lanes, 0, CH // 2, True, 3) for lanes in outer),
        *((2, lanes, CH // 2, CH // 2, False, 3) for lanes in outer),
    )

    def x_copy(f, k, arriving=False):
        sent, lanes, low, size, to_right, received = x_table[k]
        place = bufs[f].at[rows_of(chips[received if arriving else sent], core, low, size), lanes]
        return remote(place, place, x_send.at[f, k], x_recv.at[f, k], right if to_right else left)

    def e_copy(f, j, down, arriving=False):
        rows = rows_of(chips[j], core)
        k = 2 * j + down
        src = bufs[f].at[rows, last if down else first]
        dst = bufs[f].at[rows, top if down else bottom]
        device = (jnp.minimum(tile + 1, TILES - 1) if down else jnp.maximum(tile - 1, 0), chan)
        return remote(dst if arriving else src, dst, e_send.at[f, k], e_recv.at[f, k], device)

    def e_start(f, j, down):
        @pl.when(has_down if down else has_up)
        def _():
            e_copy(f, j, down).start()

    def e_wait_recv(f, j, down):
        @pl.when(has_up if down else has_down)
        def _():
            e_copy(f, j, down, True).wait_recv()

    d_table = (
        (0, pl.ds(0, LANES)),
        (1, pl.ds(0, LANES)),
        (2, pl.ds(0, LANES)),
        (3, quarters[0]),
        (3, quarters[3]),
        (3, top),
        (3, bottom),
        (3, middle),
    )

    def d_copy(f, k, arriving=False):
        j, lanes = d_table[k]
        place = bufs[f].at[rows_of(chips[j], 1 - core if arriving else core), lanes]
        return remote(place, place, d_send.at[f, k], d_recv.at[f, k], sibling)

    def own_start(f, second):
        if second:
            x_copy(f, 2).start()
            x_copy(f, 5).start()
            return
        for k in (0, 3, 1, 4):
            x_copy(f, k).start()
        e_start(f, 0, 0)
        e_start(f, 0, 1)

    def pass_on(f, j):
        e_wait_recv(f, j, 1)
        e_wait_recv(f, j, 0)
        d_copy(f, j).start()

    def near_first(f, onward):
        for part in range(2):
            for side in range(2):
                x_copy(f, 3 * side + part, True).wait_recv()
                if onward:
                    x_copy(f, 6 + 3 * side + part).start()
                e_start(f, 1 + side, part)

    def near_second(f, onward):
        for side in range(2):
            x_copy(f, 3 * side + 2, True).wait_recv()
            if onward:
                x_copy(f, 8 + 3 * side).start()

    def far_first(f):
        for part in range(2):
            x_copy(f, 6 + part, True).wait_recv()
            x_copy(f, 9 + part, True).wait_recv()
            e_start(f, 3, part)
            d_copy(f, 3 + part).start()

    def far_second(f):
        x_copy(f, 8, True).wait_recv()
        x_copy(f, 11, True).wait_recv()
        d_copy(f, 7).start()

    def far_edges(f):
        e_wait_recv(f, 3, 1)
        d_copy(f, 5).start()
        e_wait_recv(f, 3, 0)
        d_copy(f, 6).start()

    def d_wait(f, j):
        for k in range(len(d_table)):
            if d_table[k][0] == j:
                d_copy(f, k, True).wait_recv()

    def products(buf, weights, pairs, start, size):
        total = None
        for r in range(3):
            lanes = pl.ds(start + r * COLS, size)
            taps = pl.ds(r * 3 * CH, 3 * CH)
            if pairs is None:
                lhs, rhs = weights[taps, :], buf[:, lanes]
            else:
                lhs = [weights[taps, pair_of(p)] for p in pairs]
                rhs = [buf[pair_of(p), lanes] for p in pairs]
                lhs = lhs[0] if len(lhs) == 1 else jnp.concatenate(lhs, axis=1)
                rhs = rhs[0] if len(rhs) == 1 else jnp.concatenate(rhs, axis=0)
            term = jnp.dot(lhs, rhs, preferred_element_type=F32)
            total = term if total is None else total + term
        return total

    def conv_pass(buf, weights, pairs, start):
        for block in range(2):
            lanes = pl.ds(block * BLOCK, BLOCK)
            terms = products(buf, weights, pairs, block * BLOCK, BLOCK)
            zbuf[:, lanes] = terms if start else zbuf[:, lanes] + terms

    with jax.named_scope("prepare"):
        inward[0].wait()
        ga[own, inner] = gout_ref[...].reshape(CH, CELLS)
        for buf in bufs:
            for chip in chips:
                @pl.when(tile == 0)
                def _(buf=buf, chip=chip):
                    buf[rows_of(chip, core), top] = jnp.zeros((CH, COLS), BF16)

                @pl.when(tile == TILES - 1)
                def _(buf=buf, chip=chip):
                    buf[rows_of(chip, core), bottom] = jnp.zeros((CH, COLS), BF16)

    with jax.named_scope("barrier_wait"):
        pl.semaphore_wait(barrier, TILES + CHANS - 2)
    with jax.named_scope("first_sends"):
        own_start(G, 0)
        own_start(G, 1)

    with jax.named_scope("stations"):
        marks = jnp.concatenate([owner_ref[...], valid_ref[...], jnp.zeros((6, SHARD), jnp.int32)], axis=0)
        columns = marks.astype(F32).T
        owners, usable = columns[:, 0:1].astype(jnp.int32), columns[:, 1:2] == 1.0
        tile_of = lax.broadcasted_iota(jnp.int32, (SHARD, 128), 1)
        named = jnp.where((owners == tile_of) & usable, 1.0, 0.0)
        lower = lax.broadcasted_iota(jnp.int32, (SHARD, SHARD), 0) >= lax.broadcasted_iota(jnp.int32, (SHARD, SHARD), 1)
        counts = jnp.dot(jnp.where(lower, 1.0, 0.0).astype(BF16), named.astype(BF16), preferred_element_type=F32)
        rank = jnp.sum(counts * named, axis=1, keepdims=True).astype(jnp.int32) - 1
        slot = jnp.where(usable, owners * CAP + rank, -1)
        cells = cell_ref[...]
        sub = lax.broadcasted_iota(jnp.int32, (PACK - CH, SHARD), 0)
        places = jnp.where(sub == 0, cells // COLS, jnp.where(sub == 1, cells % COLS, 0))
        rowed = jnp.concatenate([feats_ref[...], places.astype(F32).astype(BF16)], axis=0)
        lane = lax.broadcasted_iota(jnp.int32, (PACK // 2, 128), 1)
        for part in range(2):
            number = lax.broadcasted_iota(jnp.int32, (SHARD, 512), 1) + part * 512
            chosen = jnp.where(slot == number, 1.0, 0.0).astype(BF16)
            sent = jnp.dot(rowed, chosen, preferred_element_type=F32)
            for k in range(4):
                upper, lower = sent[: PACK // 2, k * 128 : (k + 1) * 128], sent[PACK // 2 :, k * 128 : (k + 1) * 128]
                to = 2 * (part * 4 + k)
                packed[to] = jnp.where(lane < CAP, upper, pltpu.roll(lower, CAP, 1)).astype(BF16)
                packed[to + 1] = jnp.where(lane < CAP, pltpu.roll(upper, CAP, 1), lower).astype(BF16)
        landed[tile] = packed[tile]

    def s_copy(step, arriving=False):
        other = (tile + step) % TILES
        place = landed.at[(tile + TILES - step) % TILES]
        if arriving:
            return remote(place, place, s_send.at[step], s_recv.at[step], (other, chan))
        return remote(packed.at[other], landed.at[tile], s_send.at[step], s_recv.at[step], (other, chan))

    def w_copy(step, arriving=False):
        other = (chan + step) % CHANS
        rows = pl.ds(pl.multiple_of(z * 16, 16), 16)
        place = wb.at[(chan + CHANS - step) % CHANS, rows]
        if arriving:
            return remote(place, place, w_send.at[step], w_recv.at[step], (tile, other))
        return remote(b2.at[other, rows], wb.at[chan, rows], w_send.at[step], w_recv.at[step], (tile, other))

    def v_copy(step, arriving=False):
        other = y * 4 + (z + step) % 4
        quarter = (z + 4 - step) % 4 if arriving else z
        place = wb.at[:, pl.ds(pl.multiple_of(quarter * 16, 16), 16)]
        return remote(place, place, v_send.at[step], v_recv.at[step], (other, chan))

    for step in range(1, TILES):
        s_copy(step).start()

    with jax.named_scope("weight_pieces"):
        inward[1].wait()
        lane = lax.broadcasted_iota(jnp.int32, (CH, 128), 1)
        for chip in range(4):
            taps = [w2_ref[pl.ds((8 - n) * CH, CH), pl.ds(chip * 128, 128)].astype(F32) for n in range(9)]
            turned = [pltpu.roll(tap, CH, 1) for tap in taps]
            for k in range(5):
                n = 2 * k
                even = jnp.where(lane < CH, taps[n], turned[n + 1] if n < 8 else 0.0)
                odd = jnp.where(lane < CH, turned[n], taps[n + 1] if n < 8 else 0.0)
                b2[2 * chip, :, pl.ds(k * 128, 128)] = even.astype(BF16)
                b2[2 * chip + 1, :, pl.ds(k * 128, 128)] = odd.astype(BF16)
        for step in range(1, CHANS):
            w_copy(step).start()
        mine = pl.ds(pl.multiple_of(z * 16, 16), 16)
        wb[chan, mine] = b2[chan, mine]

    with jax.named_scope("station_wait"):
        for step in range(1, TILES):
            s_copy(step, True).wait_recv()
    with jax.named_scope("assimilate"):
        lane = lax.broadcasted_iota(jnp.int32, (PACK // 2, 128), 1)
        slabs = []
        for k in range(TILES // 2):
            even, odd = landed[2 * k].astype(F32), landed[2 * k + 1].astype(F32)
            upper = jnp.where(lane < CAP, even, pltpu.roll(odd, CAP, 1))
            lower = jnp.where(lane < CAP, pltpu.roll(even, CAP, 1), odd)
            slabs.append(jnp.concatenate([upper, lower], axis=0))
        stations = jnp.concatenate(slabs, axis=1)
        slots = stations.shape[1]
        station_row, station_col = stations[CH : CH + 1], stations[CH + 1 : CH + 2]
        spread = lax.broadcasted_iota(jnp.int32, (COLS, slots), 0).astype(F32)
        col_hot = jnp.where(station_col == spread, 1.0, 0.0).astype(BF16)
        features = stations[:CH]
        for i in range(ROWS):
            masked[pl.ds(i * CH, CH), :] = jnp.where(station_row == float(i), features, 0.0).astype(BF16)
        inward[2].wait()
        background = grid_ref[...].reshape(CH, CELLS)
        for number, quarter in enumerate((0, 3, 1, 2)):
            rows = pl.ds(quarter * 256, 256)
            sums = lax.dot_general(masked[rows, :], col_hot, NT, preferred_element_type=F32)
            for k in range(4):
                i = quarter * 4 + k
                value = background[:, i * COLS : (i + 1) * COLS].astype(F32) + sums[k * CH : (k + 1) * CH]
                aa[own, pl.ds((i + 1) * COLS, COLS)] = value.astype(BF16)
            if number % 2:
                own_start(A, number // 2)

    with jax.named_scope("pass_on_0"):
        pass_on(G, 0)
        pass_on(A, 0)
    with jax.named_scope("wait_A0"):
        d_wait(A, 0)
    with jax.named_scope("conv1_pass1"):
        inward[3].wait()
        conv_pass(aa, w1_ref, [chips[0]], True)
    with jax.named_scope("weights_round"):
        for step in range(1, CHANS):
            w_copy(step, True).wait_recv()
        for step in range(1, 4):
            v_copy(step).start()
    with jax.named_scope("near_G1"):
        near_first(G, False)
    with jax.named_scope("near_A1"):
        near_first(A, True)
    with jax.named_scope("near_G2"):
        near_second(G, False)
    with jax.named_scope("near_A2"):
        near_second(A, True)
    with jax.named_scope("pass_on_A12"):
        pass_on(A, 1)
        pass_on(A, 2)
    with jax.named_scope("far_A1"):
        far_first(A)
    with jax.named_scope("wait_A12"):
        d_wait(A, 1)
        d_wait(A, 2)
    with jax.named_scope("conv1_pass2"):
        conv_pass(aa, w1_ref, [chips[1], chips[2]], False)
    with jax.named_scope("far_A2"):
        far_second(A)
        for k in (6, 9, 7, 10, 8, 11):
            x_copy(G, k).start()
    with jax.named_scope("far_A_edges"):
        far_edges(A)
        pass_on(G, 1)
        pass_on(G, 2)
    with jax.named_scope("wait_A3"):
        d_wait(A, 3)
    with jax.named_scope("conv1_pass3"):
        for number, (start, size) in enumerate(((0, 1024), (3072, 1024), (1024, BLOCK))):
            lanes = pl.ds(start, size)
            value = neighbour_sum(zbuf[:, lanes] + products(aa, w1_ref, [chips[3]], start, size))
            hidden_pre[:, lanes] = value
            hidden = value * (1.0 / (1.0 + jnp.exp(-value)))
            ha[own, pl.ds(start + COLS, size)] = hidden.astype(BF16)
            if number:
                own_start(H, number - 1)

    groups = ((0, 1, 2), (3,))
    group_lanes = (pl.ds(0, 384), pl.ds(384, 128))

    def weight_terms(group):
        for r in range(3):
            lanes = pl.ds((2 - r) * COLS, CELLS)
            against = [ga[pair_of(chips[j]), lanes] for j in groups[group]]
            against = against[0] if len(against) == 1 else jnp.concatenate(against, axis=0)
            term = lax.dot_general(h3[...], against, NT, preferred_element_type=F32).astype(BF16)
            for part in range(2):
                gw_out[part, r, :, group_lanes[group]] = term[part * 96 : (part + 1) * 96]

    collects = z // 2 == core
    owns = collects & (y == x)

    def one_copy(part, group):
        target = 2 * core + part
        slot = jnp.maximum((target + 4 - z) % 4 - 1, 0)
        return remote(
            gw_out.at[part, :, :, group_lanes[group]],
            gw_one.at[slot, :, :, group_lanes[group]],
            one_send.at[part, group],
            one_recv.at[slot, group],
            (y * 4 + target, chan),
        )

    def one_start(group):
        for part in range(2):
            @pl.when(2 * core + part != z)
            def _(part=part):
                one_copy(part, group).start()

    def two_copy(group):
        slot = jnp.maximum((x + 4 - y) % 4 - 1, 0)
        return remote(
            gw_mid.at[:, :, group_lanes[group]],
            gw_two.at[slot, :, :, group_lanes[group]],
            two_send.at[group],
            two_recv.at[slot, group],
            (x * 4 + z, chan),
        )

    def slot_wait(buf, recv, slot, group):
        place = buf.at[slot, :, :, group_lanes[group]]
        remote(place, place, recv.at[slot, group], recv.at[slot, group], (tile, chan)).wait_recv()

    def collect(group):
        @pl.when(collects)
        def _():
            for slot in range(3):
                slot_wait(gw_one, one_recv, slot, group)
            lanes = group_lanes[group]
            total = gw_out[z % 2, :, :, lanes].astype(F32)
            for slot in range(3):
                total = total + gw_one[slot, :, :, lanes].astype(F32)
            gw_mid[:, :, lanes] = total.astype(BF16)

            @pl.when(y != x)
            def _():
                two_copy(group).start()

    def finish(group):
        @pl.when(owns)
        def _():
            for slot in range(3):
                slot_wait(gw_two, two_recv, slot, group)
            lanes = group_lanes[group]
            total = gw_mid[:, :, lanes].astype(F32)
            for slot in range(3):
                total = total + gw_two[slot, :, :, lanes].astype(F32)
            lane = lax.broadcasted_iota(jnp.int32, (144, 128), 1)
            for k, j in enumerate(groups[group]):
                both = total[:, :, k * 128 : (k + 1) * 128].reshape(288, 128)
                upper, lower = both[:144], both[144:]
                gw_fin[j, 0] = jnp.where(lane < CH, upper, pltpu.roll(lower, CH, 1)).astype(BF16)
                gw_fin[j, 1] = jnp.where(lane < CH, pltpu.roll(upper, CH, 1), lower).astype(BF16)
                for which in range(2):
                    if j == 0:
                        @pl.when(core != which)
                        def _(j=j, which=which):
                            three_copy(j, which).start()
                    else:
                        three_copy(j, which).start()
            if group == 0:
                gw_land[...] = gw_fin[0, core]

    def three_copy(j, which):
        return remote(
            gw_fin.at[j, which],
            gw_land,
            three_send.at[j, which],
            three_recv.at[0],
            (tile, chips[j] * 2 + which),
        )

    with jax.named_scope("hidden_columns"):
        mine_h = ha[own, inner].astype(F32)
        moved = (shifted(mine_h, 1), mine_h, shifted(mine_h, -1))
        for part in range(2):
            for q in range(3):
                h3[pl.ds(part * 96 + q * PART, PART), :] = moved[q][part * PART : (part + 1) * PART].astype(BF16)
    with jax.named_scope("weight_terms_0"):
        d_wait(G, 0)
        d_wait(G, 1)
        d_wait(G, 2)
        weight_terms(0)
        one_start(0)
    with jax.named_scope("pass_on_H0"):
        pass_on(H, 0)
    with jax.named_scope("conv2_pass1"):
        d_wait(H, 0)
        conv_pass(ha, w2_ref, [chips[0]], True)
    with jax.named_scope("near_H1"):
        near_first(H, True)
    with jax.named_scope("far_G"):
        far_first(G)
        far_second(G)
        far_edges(G)
    with jax.named_scope("collect_0"):
        collect(0)
    with jax.named_scope("weight_terms_1"):
        d_wait(G, 3)
        weight_terms(1)
        one_start(1)
    with jax.named_scope("near_H2"):
        near_second(H, True)
        pass_on(H, 1)
        pass_on(H, 2)
    with jax.named_scope("turn_weights"):
        for step in range(1, 4):
            v_copy(step, True).wait_recv()
        for s in range(CHANS // 2):
            two = jnp.concatenate([wb[2 * s], wb[2 * s + 1]], axis=0).astype(F32)
            wbt[:, pl.ds(s * 128, 128)] = two.T.astype(BF16)
    with jax.named_scope("far_H1"):
        far_first(H)
    with jax.named_scope("collect_1"):
        collect(1)
    with jax.named_scope("grad_hidden"):
        for block in range(2):
            lanes = pl.ds(block * BLOCK, BLOCK)
            grad_act = neighbour_sum(products(ga, wbt, None, block * BLOCK, BLOCK))
            value = hidden_pre[:, lanes]
            s = 1.0 / (1.0 + jnp.exp(-value))
            result = (grad_act * s * (1.0 + value * (1.0 - s))).astype(BF16)
            gh_ref[:, block * 8 : block * 8 + 8, :] = result.reshape(CH, 8, COLS)
    with jax.named_scope("conv2_pass2"):
        d_wait(H, 1)
        d_wait(H, 2)
        conv_pass(ha, w2_ref, [chips[1], chips[2]], False)
    with jax.named_scope("finish_0"):
        finish(0)
    with jax.named_scope("finish_1"):
        finish(1)
    with jax.named_scope("far_H2"):
        far_second(H)
    with jax.named_scope("far_H_edges"):
        far_edges(H)
    with jax.named_scope("wait_H3"):
        d_wait(H, 3)
    with jax.named_scope("conv2_pass3"):
        for block in range(2):
            lanes = pl.ds(block * BLOCK, BLOCK)
            branch = neighbour_sum(zbuf[:, lanes] + products(ha, w2_ref, [chips[3]], block * BLOCK, BLOCK))
            result = (aa[own, pl.ds(block * BLOCK + COLS, BLOCK)].astype(F32) + branch).astype(BF16)
            out_ref[:, block * 8 : block * 8 + 8, :] = result.reshape(CH, 8, COLS)
    with jax.named_scope("grad_weight"):
        @pl.when(jnp.logical_not(owns))
        def _():
            remote(gw_land, gw_land, three_recv.at[0], three_recv.at[0], (tile, chan)).wait_recv()

        piece = gw_land[...].astype(F32)
        sides = (piece[:, :CH].astype(BF16), pltpu.roll(piece, CH, 1)[:, :CH].astype(BF16))
        for n in range(18):
            rows = sides[n // 9][(n % 9) * 16 : (n % 9) * 16 + 16]
            gw_ref[n // 6, n % 6 // 2, pl.ds(n % 2 * 16, 16), :] = rows

    with jax.named_scope("sends_done"):
        for f in (G, A, H):
            for k in range(len(x_table)):
                x_copy(f, k).wait_send()
            for k in range(len(d_table)):
                d_copy(f, k).wait_send()
            for j in range(4):
                @pl.when(has_up)
                def _(f=f, j=j):
                    e_copy(f, j, 0).wait_send()

                @pl.when(has_down)
                def _(f=f, j=j):
                    e_copy(f, j, 1).wait_send()

        for step in range(1, TILES):
            s_copy(step).wait_send()
        for step in range(1, CHANS):
            w_copy(step).wait_send()
        for step in range(1, 4):
            v_copy(step).wait_send()
        for group in range(2):
            for part in range(2):
                @pl.when(2 * core + part != z)
                def _(part=part, group=group):
                    one_copy(part, group).wait_send()

            @pl.when(collects & (y != x))
            def _(group=group):
                two_copy(group).wait_send()

        @pl.when(owns)
        def _():
            for j in range(4):
                for which in range(2):
                    if j == 0:
                        @pl.when(core != which)
                        def _(j=j, which=which):
                            three_copy(j, which).wait_send()
                    else:
                        three_copy(j, which).wait_send()


def hand_over(out_from, gw_from, gh_from, out_to, gw_to, gh_to, out_via, gw_via, gh_via, sems):
    parts = [pl.ds(k * 16, 16) for k in range(4)]
    ways = [(gw_from, gw_via, gw_to)]
    for part in parts:
        ways.append((out_from.at[part], out_via.at[part], out_to.at[part]))
        ways.append((gh_from.at[part], gh_via.at[part], gh_to.at[part]))
    inward = [pltpu.make_async_copy(src, via, sems.at[0, k]) for k, (src, via, _) in enumerate(ways)]
    outward = [pltpu.make_async_copy(via, dst, sems.at[1, k]) for k, (_, via, dst) in enumerate(ways)]
    for copy in inward:
        copy.start()
    for arrive, leave in zip(inward, outward):
        arrive.wait()
        leave.start()
    for copy in outward:
        copy.wait()


def local(grid, station_feats, owner_tile, station_cell, valid, conv_first, conv_second, grad_out):
    w1 = conv_first.transpose(0, 1, 3, 2).reshape(9 * CH, ALL)
    w2 = conv_second.transpose(0, 1, 3, 2).reshape(9 * CH, ALL)
    whole = pl.BlockSpec(memory_space=pl.ANY)
    vmem = pl.BlockSpec(memory_space=pltpu.VMEM)
    dma = pltpu.SemaphoreType.DMA
    results = pl.pallas_call(
        kernel,
        out_shape=(
            jax.ShapeDtypeStruct((CH, ROWS, COLS), BF16),
            jax.ShapeDtypeStruct((3, 3, PART, CH), BF16),
            jax.ShapeDtypeStruct((CH, ROWS, COLS), BF16),
        ),
        in_specs=[vmem] * 4 + [whole] * 4,
        out_specs=(vmem,) * 3,
        scratch_shapes=[
            pltpu.VMEM((CH, ROWS, COLS), BF16),
            pltpu.VMEM((CH, ROWS, COLS), BF16),
            pltpu.VMEM((9 * CH, ALL), BF16),
            pltpu.VMEM((9 * CH, ALL), BF16),
            dma((4,)),
            pltpu.VMEM((ALL, LANES), BF16),
            pltpu.VMEM((ALL, LANES), BF16),
            pltpu.VMEM((ALL, LANES), BF16),
            pltpu.VMEM((3 * CH, CELLS), F32),
            pltpu.VMEM((CH, CELLS), F32),
            pltpu.VMEM((3 * CH, CELLS), BF16),
            pltpu.VMEM((CHANS, CH, 10 * CH), BF16),
            pltpu.VMEM((CHANS, CH, 10 * CH), BF16),
            pltpu.VMEM((10 * CH, ALL), BF16),
            pltpu.VMEM((TILES, PACK // 2, 128), BF16),
            pltpu.VMEM((TILES, PACK // 2, 128), BF16),
            pltpu.VMEM((ROWS * CH, TILES * CAP), BF16),
            pltpu.VMEM((2, 3, 96, ALL), BF16),
            pltpu.VMEM((3, 3, 96, ALL), BF16),
            pltpu.VMEM((3, 96, ALL), BF16),
            pltpu.VMEM((3, 3, 96, ALL), BF16),
            pltpu.VMEM((4, 2, 144, 128), BF16),
            pltpu.VMEM((144, 128), BF16),
            dma((3, 12)), dma((3, 12)), dma((3, 8)), dma((3, 8)), dma((3, 8)), dma((3, 8)),
            dma((TILES,)), dma((TILES,)), dma((CHANS,)), dma((CHANS,)), dma((4,)), dma((4,)),
            dma((2, 2)), dma((3, 2)), dma((2,)), dma((3, 2)), dma((4, 2)), dma((1,)),
        ],
        compiler_params=pltpu.CompilerParams(
            collective_id=0, has_side_effects=True, vmem_limit_bytes=56 * 1024 * 1024
        ),
    )(
        station_feats,
        owner_tile.reshape(1, SHARD),
        valid.reshape(1, SHARD),
        station_cell.reshape(1, SHARD),
        grad_out,
        grid,
        w1,
        w2,
    )
    return pl.pallas_call(
        hand_over,
        out_shape=tuple(jax.ShapeDtypeStruct(result.shape, result.dtype) for result in results),
        in_specs=[whole] * 3,
        out_specs=(whole,) * 3,
        scratch_shapes=[*(pltpu.VMEM(result.shape, BF16) for result in results), dma((2, 9))],
    )(*results)


def solution(mesh):
    return jax.shard_map(
        local,
        mesh=mesh,
        in_specs=(
            P("chan", "tile", None),
            P("chan", "tile"),
            P("tile", None),
            P("tile"),
            P("tile"),
            P(None, None, None, "chan"),
            P(None, None, None, "chan"),
            P("chan", "tile", None),
        ),
        out_specs=(P("chan", "tile", None), P(None, None, "tile", "chan"), P("chan", "tile", None)),
        check_vma=False,
    )
```

```python
import jax
import jax.numpy as jnp
from jax import lax
from jax.experimental import pallas as pl
from jax.experimental.pallas import tpu as pltpu
from jax.sharding import PartitionSpec as P

MESH = pl.DeviceIdType.MESH
BF16 = jnp.bfloat16
F32 = jnp.float32

CH = 64
ROWS = 16
COLS = 256
CELLS = ROWS * COLS
LANES = CELLS + 2 * COLS
BLOCK = CELLS // 2
TILES = 16
CHANS = 8
ALL = CH * CHANS
SHARD = 512
CAP = 64
PACK = 96
PART = 32
NT = (((1,), (1,)), ((), ()))

G, A, H = 0, 1, 2


def shifted(values, by):
    lanes = values.shape[1]
    col = lax.broadcasted_iota(jnp.int32, values.shape, 1) % COLS
    if by == 1:
        return jnp.where(col == 0, 0.0, pltpu.roll(values, 1, 1))
    return jnp.where(col == COLS - 1, 0.0, pltpu.roll(values, lanes - 1, 1))


def neighbour_sum(z):
    return z[CH : 2 * CH] + shifted(z[:CH], 1) + shifted(z[2 * CH :], -1)


def kernel(
    feats_ref, owner_ref, valid_ref, cell_ref, gout_hbm, grid_hbm, w1_hbm, w2_hbm,
    out_ref, gw_ref, gh_ref,
    gout_ref, grid_ref, w1_ref, w2_ref, in_sem, ga, aa, ha, zbuf, hidden_pre, h3, b2, wb, wbt, packed, passing, landed, masked,
    gw_out, gw_one, gw_mid, gw_two, gw_fin, gw_land,
    x_send, x_recv, e_send, e_recv, d_send, d_recv, s_send, s_recv, w_send, w_recv, v_send, v_recv,
    one_send, one_recv, two_send, two_recv, three_send, three_recv,
):
    tile = lax.axis_index("tile")
    chan = lax.axis_index("chan")
    x, core = chan // 2, chan % 2
    y, z = tile // 4, tile % 4
    bufs = (ga, aa, ha)
    chips = [x, (x + 3) % 4, (x + 1) % 4, (x + 2) % 4]
    right = (tile, chips[2] * 2 + core)
    left = (tile, chips[1] * 2 + core)
    sibling = (tile, x * 2 + (1 - core))
    has_up, has_down = tile > 0, tile < TILES - 1

    inward = [
        pltpu.make_async_copy(src, dst, in_sem.at[k])
        for k, (src, dst) in enumerate(
            ((gout_hbm, gout_ref), (w2_hbm, w2_ref), (grid_hbm, grid_ref), (w1_hbm, w1_ref))
        )
    ]
    for copy in inward:
        copy.start()

    barrier = pltpu.get_barrier_semaphore()
    across_up, across_down = has_up & (z == 0), has_down & (z == 3)
    for step in range(1, 4):
        for peer in (y * 4 + (z + step) % 4, (y + step) % 4 * 4 + z):
            pl.semaphore_signal(barrier, inc=1, device_id=(peer, chan), device_id_type=MESH)
    for across, peer in ((across_up, jnp.maximum(tile - 1, 0)), (across_down, jnp.minimum(tile + 1, TILES - 1))):
        @pl.when(across)
        def _(peer=peer):
            pl.semaphore_signal(barrier, inc=1, device_id=(peer, chan), device_id_type=MESH)

    for step in range(1, CHANS):
        pl.semaphore_signal(barrier, inc=1, device_id=(tile, (chan + step) % CHANS), device_id_type=MESH)

    def rows_of(chip, which, low=0, size=CH):
        return pl.ds(pl.multiple_of(chip * (2 * CH) + which * CH + low, size), size)

    def pair_of(chip):
        return pl.ds(pl.multiple_of(chip * (2 * CH), 2 * CH), 2 * CH)

    own = rows_of(x, core)
    quarters = [pl.ds(COLS + q * 1024, 1024) for q in range(4)]
    middle = pl.ds(COLS + 1024, BLOCK)
    top, bottom = pl.ds(0, COLS), pl.ds(COLS + CELLS, COLS)
    first, last = pl.ds(COLS, COLS), pl.ds(CELLS, COLS)
    inner = pl.ds(COLS, CELLS)

    def remote(src, dst, send, recv, device):
        return pltpu.make_async_remote_copy(
            src_ref=src, dst_ref=dst, send_sem=send, recv_sem=recv, device_id=device, device_id_type=MESH
        )

    outer = (quarters[0], quarters[3], middle)
    x_table = (
        *((0, lanes, 0, CH, True, 1) for lanes in outer),
        *((0, lanes, 0, CH, False, 2) for lanes in outer),
        *((1, lanes, 0, CH // 2, True, 3) for lanes in outer),
        *((2, lanes, CH // 2, CH // 2, False, 3) for lanes in outer),
    )

    def x_copy(f, k, arriving=False):
        sent, lanes, low, size, to_right, received = x_table[k]
        place = bufs[f].at[rows_of(chips[received if arriving else sent], core, low, size), lanes]
        return remote(place, place, x_send.at[f, k], x_recv.at[f, k], right if to_right else left)

    def e_copy(f, j, down, arriving=False):
        rows = rows_of(chips[j], core)
        k = 2 * j + down
        src = bufs[f].at[rows, last if down else first]
        dst = bufs[f].at[rows, top if down else bottom]
        device = (jnp.minimum(tile + 1, TILES - 1) if down else jnp.maximum(tile - 1, 0), chan)
        return remote(dst if arriving else src, dst, e_send.at[f, k], e_recv.at[f, k], device)

    def e_start(f, j, down):
        @pl.when(has_down if down else has_up)
        def _():
            e_copy(f, j, down).start()

    def e_wait_recv(f, j, down):
        @pl.when(has_up if down else has_down)
        def _():
            e_copy(f, j, down, True).wait_recv()

    d_parts = (quarters[0], quarters[3], top, bottom, middle)
    d_table = ((0, pl.ds(0, LANES)), *((j, lanes) for j in (1, 2, 3) for lanes in d_parts))

    def d_copy(f, k, arriving=False):
        j, lanes = d_table[k]
        place = bufs[f].at[rows_of(chips[j], 1 - core if arriving else core), lanes]
        return remote(place, place, d_send.at[f, k], d_recv.at[f, k], sibling)

    def own_start(f, second):
        if second:
            x_copy(f, 2).start()
            x_copy(f, 5).start()
            return
        for k in (0, 3, 1, 4):
            x_copy(f, k).start()
        e_start(f, 0, 0)
        e_start(f, 0, 1)

    def pass_on(f, j):
        e_wait_recv(f, j, 1)
        if j:
            d_copy(f, 5 * j - 2).start()
        e_wait_recv(f, j, 0)
        d_copy(f, 5 * j - 1 if j else 0).start()

    def near_first(f, onward):
        for part in range(2):
            for side in range(2):
                x_copy(f, 3 * side + part, True).wait_recv()
                if onward:
                    x_copy(f, 6 + 3 * side + part).start()
                e_start(f, 1 + side, part)
                d_copy(f, 5 * side + 1 + part).start()

    def near_second(f, onward):
        for side in range(2):
            x_copy(f, 3 * side + 2, True).wait_recv()
            if onward:
                x_copy(f, 8 + 3 * side).start()
            d_copy(f, 5 * side + 5).start()

    def far_first(f):
        for part in range(2):
            x_copy(f, 6 + part, True).wait_recv()
            x_copy(f, 9 + part, True).wait_recv()
            e_start(f, 3, part)
            d_copy(f, 11 + part).start()

    def far_second(f):
        x_copy(f, 8, True).wait_recv()
        x_copy(f, 11, True).wait_recv()
        d_copy(f, 15).start()

    def far_edges(f):
        pass_on(f, 3)

    def d_wait(f, j):
        for k in range(len(d_table)):
            if d_table[k][0] == j:
                d_copy(f, k, True).wait_recv()

    def d_wait_parts(f, ks):
        for k in ks:
            d_copy(f, k, True).wait_recv()

    def products(buf, weights, pairs, start, size):
        total = None
        for r in range(3):
            lanes = pl.ds(start + r * COLS, size)
            taps = pl.ds(r * 3 * CH, 3 * CH)
            if pairs is None:
                lhs, rhs = weights[taps, :], buf[:, lanes]
            else:
                lhs = [weights[taps, pair_of(p)] for p in pairs]
                rhs = [buf[pair_of(p), lanes] for p in pairs]
                lhs = lhs[0] if len(lhs) == 1 else jnp.concatenate(lhs, axis=1)
                rhs = rhs[0] if len(rhs) == 1 else jnp.concatenate(rhs, axis=0)
            term = jnp.dot(lhs, rhs, preferred_element_type=F32)
            total = term if total is None else total + term
        return total

    def conv_pass(buf, weights, pairs, start):
        for block in range(2):
            lanes = pl.ds(block * BLOCK, BLOCK)
            terms = products(buf, weights, pairs, block * BLOCK, BLOCK)
            zbuf[:, lanes] = terms if start else zbuf[:, lanes] + terms

    with jax.named_scope("prepare"):
        inward[0].wait()
        ga[own, inner] = gout_ref[...].reshape(CH, CELLS)
        for buf in bufs:
            for chip in chips:
                @pl.when(tile == 0)
                def _(buf=buf, chip=chip):
                    buf[rows_of(chip, core), top] = jnp.zeros((CH, COLS), BF16)

                @pl.when(tile == TILES - 1)
                def _(buf=buf, chip=chip):
                    buf[rows_of(chip, core), bottom] = jnp.zeros((CH, COLS), BF16)

    with jax.named_scope("barrier_wait"):
        @pl.when(across_up | across_down)
        def _():
            pl.semaphore_wait(barrier, 6 + CHANS)

        @pl.when(jnp.logical_not(across_up | across_down))
        def _():
            pl.semaphore_wait(barrier, 6 + CHANS - 1)
    with jax.named_scope("first_sends"):
        own_start(G, 0)
        own_start(G, 1)

    with jax.named_scope("stations"):
        marks = jnp.concatenate([owner_ref[...], valid_ref[...], jnp.zeros((6, SHARD), jnp.int32)], axis=0)
        columns = marks.astype(F32).T
        owners, usable = columns[:, 0:1].astype(jnp.int32), columns[:, 1:2] == 1.0
        tile_of = lax.broadcasted_iota(jnp.int32, (SHARD, 128), 1)
        named = jnp.where((owners == tile_of) & usable, 1.0, 0.0)
        lower = lax.broadcasted_iota(jnp.int32, (SHARD, SHARD), 0) >= lax.broadcasted_iota(jnp.int32, (SHARD, SHARD), 1)
        counts = jnp.dot(jnp.where(lower, 1.0, 0.0).astype(BF16), named.astype(BF16), preferred_element_type=F32)
        rank = jnp.sum(counts * named, axis=1, keepdims=True).astype(jnp.int32) - 1
        slot = jnp.where(usable, owners * CAP + rank, -1)
        cells = cell_ref[...]
        sub = lax.broadcasted_iota(jnp.int32, (PACK - CH, SHARD), 0)
        places = jnp.where(sub == 0, cells // COLS, jnp.where(sub == 1, cells % COLS, 0))
        rowed = jnp.concatenate([feats_ref[...], places.astype(F32).astype(BF16)], axis=0)
        lane = lax.broadcasted_iota(jnp.int32, (PACK // 2, 128), 1)
        for part in range(2):
            number = lax.broadcasted_iota(jnp.int32, (SHARD, 512), 1) + part * 512
            chosen = jnp.where(slot == number, 1.0, 0.0).astype(BF16)
            sent = jnp.dot(rowed, chosen, preferred_element_type=F32)
            for k in range(4):
                upper, lower = sent[: PACK // 2, k * 128 : (k + 1) * 128], sent[PACK // 2 :, k * 128 : (k + 1) * 128]
                to = 2 * (part * 4 + k)
                packed[to % 4 * 4 + to // 4] = jnp.where(lane < CAP, upper, pltpu.roll(lower, CAP, 1)).astype(BF16)
                packed[(to + 1) % 4 * 4 + (to + 1) // 4] = jnp.where(lane < CAP, pltpu.roll(upper, CAP, 1), lower).astype(BF16)
        passing[z] = packed[pl.ds(z * 4, 4)]

    def s_copy(step, arriving=False):
        other = (z + step) % 4
        place = passing.at[(z + 4 - step) % 4]
        device = (y * 4 + other, chan)
        if arriving:
            return remote(place, place, s_send.at[0, step], s_recv.at[0, step], device)
        return remote(packed.at[pl.ds(other * 4, 4)], passing.at[z], s_send.at[0, step], s_recv.at[0, step], device)

    def t_copy(step, arriving=False):
        other = (y + step) % 4
        place = landed.at[(y + 4 - step) % 4]
        device = (other * 4 + z, chan)
        if arriving:
            return remote(place, place, s_send.at[1, step], s_recv.at[1, step], device)
        return remote(passing.at[:, other], landed.at[y], s_send.at[1, step], s_recv.at[1, step], device)

    def w_copy(step, arriving=False):
        other = (chan + step) % CHANS
        rows = pl.ds(pl.multiple_of(z * 16, 16), 16)
        place = wb.at[(chan + CHANS - step) % CHANS, rows]
        if arriving:
            return remote(place, place, w_send.at[step], w_recv.at[step], (tile, other))
        return remote(b2.at[other, rows], wb.at[chan, rows], w_send.at[step], w_recv.at[step], (tile, other))

    def v_copy(step, arriving=False):
        other = y * 4 + (z + step) % 4
        quarter = (z + 4 - step) % 4 if arriving else z
        place = wb.at[:, pl.ds(pl.multiple_of(quarter * 16, 16), 16)]
        return remote(place, place, v_send.at[step], v_recv.at[step], (other, chan))

    for step in range(1, 4):
        s_copy(step).start()

    with jax.named_scope("weight_pieces"):
        inward[1].wait()
        lane = lax.broadcasted_iota(jnp.int32, (CH, 128), 1)
        for chip in range(4):
            taps = [w2_ref[pl.ds((8 - n) * CH, CH), pl.ds(chip * 128, 128)].astype(F32) for n in range(9)]
            turned = [pltpu.roll(tap, CH, 1) for tap in taps]
            for k in range(5):
                n = 2 * k
                even = jnp.where(lane < CH, taps[n], turned[n + 1] if n < 8 else 0.0)
                odd = jnp.where(lane < CH, turned[n], taps[n + 1] if n < 8 else 0.0)
                b2[2 * chip, :, pl.ds(k * 128, 128)] = even.astype(BF16)
                b2[2 * chip + 1, :, pl.ds(k * 128, 128)] = odd.astype(BF16)
        for step in range(1, CHANS):
            w_copy(step).start()
        mine = pl.ds(pl.multiple_of(z * 16, 16), 16)
        wb[chan, mine] = b2[chan, mine]

    with jax.named_scope("station_wait"):
        for step in range(1, 4):
            s_copy(step, True).wait_recv()
        for step in range(1, 4):
            t_copy(step).start()
        landed[y] = passing[:, y]
        for step in range(1, 4):
            t_copy(step, True).wait_recv()
    with jax.named_scope("assimilate"):
        lane = lax.broadcasted_iota(jnp.int32, (PACK // 2, 128), 1)
        slabs = []
        for k in range(TILES // 2):
            even, odd = landed[k // 2, k % 2 * 2].astype(F32), landed[k // 2, k % 2 * 2 + 1].astype(F32)
            upper = jnp.where(lane < CAP, even, pltpu.roll(odd, CAP, 1))
            lower = jnp.where(lane < CAP, pltpu.roll(even, CAP, 1), odd)
            slabs.append(jnp.concatenate([upper, lower], axis=0))
        stations = jnp.concatenate(slabs, axis=1)
        slots = stations.shape[1]
        station_row, station_col = stations[CH : CH + 1], stations[CH + 1 : CH + 2]
        spread = lax.broadcasted_iota(jnp.int32, (COLS, slots), 0).astype(F32)
        col_hot = jnp.where(station_col == spread, 1.0, 0.0).astype(BF16)
        features = stations[:CH]
        for i in range(ROWS):
            masked[pl.ds(i * CH, CH), :] = jnp.where(station_row == float(i), features, 0.0).astype(BF16)
        inward[2].wait()
        background = grid_ref[...].reshape(CH, CELLS)
        for number, quarter in enumerate((0, 3, 1, 2)):
            rows = pl.ds(quarter * 256, 256)
            sums = lax.dot_general(masked[rows, :], col_hot, NT, preferred_element_type=F32)
            for k in range(4):
                i = quarter * 4 + k
                value = background[:, i * COLS : (i + 1) * COLS].astype(F32) + sums[k * CH : (k + 1) * CH]
                aa[own, pl.ds((i + 1) * COLS, COLS)] = value.astype(BF16)
            if number % 2:
                own_start(A, number // 2)

    with jax.named_scope("pass_on_0"):
        pass_on(G, 0)
        pass_on(A, 0)
    with jax.named_scope("wait_A0"):
        d_wait(A, 0)
    with jax.named_scope("conv1_pass1"):
        inward[3].wait()
        conv_pass(aa, w1_ref, [chips[0]], True)
    with jax.named_scope("weights_round"):
        for step in range(1, CHANS):
            w_copy(step, True).wait_recv()
        for step in range(1, 4):
            v_copy(step).start()
    with jax.named_scope("near_G1"):
        near_first(G, False)
    with jax.named_scope("near_A1"):
        near_first(A, True)
    with jax.named_scope("near_G2"):
        near_second(G, False)
    with jax.named_scope("near_A2"):
        near_second(A, True)
    with jax.named_scope("pass_on_A12"):
        pass_on(A, 1)
        pass_on(A, 2)
    with jax.named_scope("far_A1"):
        far_first(A)
    with jax.named_scope("wait_A12"):
        d_wait(A, 1)
        d_wait(A, 2)
    with jax.named_scope("conv1_pass2"):
        conv_pass(aa, w1_ref, [chips[1], chips[2]], False)
    with jax.named_scope("far_A2"):
        far_second(A)
        for k in (6, 9, 7, 10, 8, 11):
            x_copy(G, k).start()
    with jax.named_scope("far_A_edges"):
        far_edges(A)
        pass_on(G, 1)
        pass_on(G, 2)
    spans = ((0, 3 * COLS), (13 * COLS, 3 * COLS), (3 * COLS, 10 * COLS))

    with jax.named_scope("conv1_pass3"):
        d_wait_parts(A, (11, 12, 13, 14))
        for number, (start, size) in enumerate(spans):
            if number == 2:
                d_wait_parts(A, (15,))
            lanes = pl.ds(start, size)
            value = neighbour_sum(zbuf[:, lanes] + products(aa, w1_ref, [chips[3]], start, size))
            hidden_pre[:, lanes] = value
            hidden = value * (1.0 / (1.0 + jnp.exp(-value)))
            ha[own, pl.ds(start + COLS, size)] = hidden.astype(BF16)
        own_start(H, 0)

    groups = ((0, 1, 2), (3,))
    group_lanes = (pl.ds(0, 384), pl.ds(384, 128))

    def weight_terms(group):
        for r in range(3):
            lanes = pl.ds((2 - r) * COLS, CELLS)
            against = [ga[pair_of(chips[j]), lanes] for j in groups[group]]
            against = against[0] if len(against) == 1 else jnp.concatenate(against, axis=0)
            term = lax.dot_general(h3[...], against, NT, preferred_element_type=F32).astype(BF16)
            for part in range(2):
                gw_out[part, r, :, group_lanes[group]] = term[part * 96 : (part + 1) * 96]

    collects = z // 2 == core
    owns = collects & (y == x)

    def one_copy(part, group):
        target = 2 * core + part
        slot = jnp.maximum((target + 4 - z) % 4 - 1, 0)
        return remote(
            gw_out.at[part, :, :, group_lanes[group]],
            gw_one.at[slot, :, :, group_lanes[group]],
            one_send.at[part, group],
            one_recv.at[slot, group],
            (y * 4 + target, chan),
        )

    def one_start(group):
        for part in range(2):
            @pl.when(2 * core + part != z)
            def _(part=part):
                one_copy(part, group).start()

    def two_copy(group):
        slot = jnp.maximum((x + 4 - y) % 4 - 1, 0)
        return remote(
            gw_mid.at[:, :, group_lanes[group]],
            gw_two.at[slot, :, :, group_lanes[group]],
            two_send.at[group],
            two_recv.at[slot, group],
            (x * 4 + z, chan),
        )

    def slot_wait(buf, recv, slot, group):
        place = buf.at[slot, :, :, group_lanes[group]]
        remote(place, place, recv.at[slot, group], recv.at[slot, group], (tile, chan)).wait_recv()

    def collect(group):
        @pl.when(collects)
        def _():
            for slot in range(3):
                slot_wait(gw_one, one_recv, slot, group)
            lanes = group_lanes[group]
            total = gw_out[z % 2, :, :, lanes].astype(F32)
            for slot in range(3):
                total = total + gw_one[slot, :, :, lanes].astype(F32)
            gw_mid[:, :, lanes] = total.astype(BF16)

            @pl.when(y != x)
            def _():
                two_copy(group).start()

    def finish(group):
        @pl.when(owns)
        def _():
            for slot in range(3):
                slot_wait(gw_two, two_recv, slot, group)
            lanes = group_lanes[group]
            total = gw_mid[:, :, lanes].astype(F32)
            for slot in range(3):
                total = total + gw_two[slot, :, :, lanes].astype(F32)
            lane = lax.broadcasted_iota(jnp.int32, (144, 128), 1)
            for k, j in enumerate(groups[group]):
                both = total[:, :, k * 128 : (k + 1) * 128].reshape(288, 128)
                upper, lower = both[:144], both[144:]
                gw_fin[j, 0] = jnp.where(lane < CH, upper, pltpu.roll(lower, CH, 1)).astype(BF16)
                gw_fin[j, 1] = jnp.where(lane < CH, pltpu.roll(upper, CH, 1), lower).astype(BF16)
                for which in range(2):
                    if j == 0:
                        @pl.when(core != which)
                        def _(j=j, which=which):
                            three_copy(j, which).start()
                    else:
                        three_copy(j, which).start()
            if group == 0:
                gw_land[...] = gw_fin[0, core]

    def three_copy(j, which):
        return remote(
            gw_fin.at[j, which],
            gw_land,
            three_send.at[j, which],
            three_recv.at[0],
            (tile, chips[j] * 2 + which),
        )

    with jax.named_scope("hidden_columns"):
        mine_h = ha[own, inner].astype(F32)
        moved = (shifted(mine_h, 1), mine_h, shifted(mine_h, -1))
        for part in range(2):
            for q in range(3):
                h3[pl.ds(part * 96 + q * PART, PART), :] = moved[q][part * PART : (part + 1) * PART].astype(BF16)
    with jax.named_scope("weight_terms_0"):
        d_wait(G, 0)
        d_wait(G, 1)
        d_wait(G, 2)
        weight_terms(0)
    with jax.named_scope("pass_on_H0"):
        pass_on(H, 0)
    with jax.named_scope("far_G"):
        far_first(G)
        far_second(G)
        own_start(H, 1)
        one_start(0)
    with jax.named_scope("conv2_pass1"):
        d_wait(H, 0)
        conv_pass(ha, w2_ref, [chips[0]], True)
    with jax.named_scope("far_G_edges"):
        far_edges(G)
    with jax.named_scope("near_H1"):
        near_first(H, True)
    with jax.named_scope("weight_terms_1"):
        d_wait(G, 3)
        weight_terms(1)
        one_start(1)
    with jax.named_scope("turn_weights"):
        for step in range(1, 4):
            v_copy(step, True).wait_recv()
        for s in range(CHANS // 2):
            two = jnp.concatenate([wb[2 * s], wb[2 * s + 1]], axis=0).astype(F32)
            wbt[:, pl.ds(s * 128, 128)] = two.T.astype(BF16)
    def grad_hidden(block):
        lanes = pl.ds(block * BLOCK, BLOCK)
        grad_act = neighbour_sum(products(ga, wbt, None, block * BLOCK, BLOCK))
        value = hidden_pre[:, lanes]
        s = 1.0 / (1.0 + jnp.exp(-value))
        result = (grad_act * s * (1.0 + value * (1.0 - s))).astype(BF16)
        gh_ref[:, block * 8 : block * 8 + 8, :] = result.reshape(CH, 8, COLS)

    with jax.named_scope("grad_hidden_0"):
        grad_hidden(0)
    with jax.named_scope("collect_0"):
        collect(0)
    with jax.named_scope("near_H2"):
        near_second(H, True)
        pass_on(H, 1)
        pass_on(H, 2)
    with jax.named_scope("grad_hidden_1"):
        grad_hidden(1)
    with jax.named_scope("collect_1"):
        collect(1)
    with jax.named_scope("far_H1"):
        far_first(H)
    with jax.named_scope("conv2_pass2"):
        d_wait(H, 1)
        d_wait(H, 2)
        conv_pass(ha, w2_ref, [chips[1], chips[2]], False)
    with jax.named_scope("far_H2"):
        far_second(H)
    with jax.named_scope("far_H_edges"):
        far_edges(H)
    with jax.named_scope("finish_0"):
        finish(0)
    with jax.named_scope("finish_1"):
        finish(1)
    with jax.named_scope("conv2_pass3"):
        d_wait_parts(H, (11, 12, 13, 14))
        for number, (start, size) in enumerate(spans):
            if number == 2:
                d_wait_parts(H, (15,))
            lanes = pl.ds(start, size)
            branch = neighbour_sum(zbuf[:, lanes] + products(ha, w2_ref, [chips[3]], start, size))
            hidden_pre[:, lanes] = aa[own, pl.ds(start + COLS, size)].astype(F32) + branch
        out_ref[...] = hidden_pre[...].astype(BF16).reshape(CH, ROWS, COLS)
    with jax.named_scope("grad_weight"):
        @pl.when(jnp.logical_not(owns))
        def _():
            remote(gw_land, gw_land, three_recv.at[0], three_recv.at[0], (tile, chan)).wait_recv()

        piece = gw_land[...].astype(F32)
        sides = (piece[:, :CH].astype(BF16), pltpu.roll(piece, CH, 1)[:, :CH].astype(BF16))
        for n in range(18):
            rows = sides[n // 9][(n % 9) * 16 : (n % 9) * 16 + 16]
            gw_ref[n // 6, n % 6 // 2, pl.ds(n % 2 * 16, 16), :] = rows

    with jax.named_scope("sends_done"):
        for f in (G, A, H):
            for k in range(len(x_table)):
                x_copy(f, k).wait_send()
            for k in range(len(d_table)):
                d_copy(f, k).wait_send()
            for j in range(4):
                @pl.when(has_up)
                def _(f=f, j=j):
                    e_copy(f, j, 0).wait_send()

                @pl.when(has_down)
                def _(f=f, j=j):
                    e_copy(f, j, 1).wait_send()

        for step in range(1, 4):
            s_copy(step).wait_send()
            t_copy(step).wait_send()
        for step in range(1, CHANS):
            w_copy(step).wait_send()
        for step in range(1, 4):
            v_copy(step).wait_send()
        for group in range(2):
            for part in range(2):
                @pl.when(2 * core + part != z)
                def _(part=part, group=group):
                    one_copy(part, group).wait_send()

            @pl.when(collects & (y != x))
            def _(group=group):
                two_copy(group).wait_send()

        @pl.when(owns)
        def _():
            for j in range(4):
                for which in range(2):
                    if j == 0:
                        @pl.when(core != which)
                        def _(j=j, which=which):
                            three_copy(j, which).wait_send()
                    else:
                        three_copy(j, which).wait_send()


def hand_over(out_from, gw_from, gh_from, out_to, gw_to, gh_to, out_via, gw_via, gh_via, sems):
    parts = [pl.ds(k * 16, 16) for k in range(4)]
    ways = [(gw_from, gw_via, gw_to)]
    for part in parts:
        ways.append((out_from.at[part], out_via.at[part], out_to.at[part]))
        ways.append((gh_from.at[part], gh_via.at[part], gh_to.at[part]))
    inward = [pltpu.make_async_copy(src, via, sems.at[0, k]) for k, (src, via, _) in enumerate(ways)]
    outward = [pltpu.make_async_copy(via, dst, sems.at[1, k]) for k, (_, via, dst) in enumerate(ways)]
    for copy in inward:
        copy.start()
    for arrive, leave in zip(inward, outward):
        arrive.wait()
        leave.start()
    for copy in outward:
        copy.wait()


def local(grid, station_feats, owner_tile, station_cell, valid, conv_first, conv_second, grad_out):
    w1 = conv_first.transpose(0, 1, 3, 2).reshape(9 * CH, ALL)
    w2 = conv_second.transpose(0, 1, 3, 2).reshape(9 * CH, ALL)
    whole = pl.BlockSpec(memory_space=pl.ANY)
    vmem = pl.BlockSpec(memory_space=pltpu.VMEM)
    dma = pltpu.SemaphoreType.DMA
    results = pl.pallas_call(
        kernel,
        out_shape=(
            jax.ShapeDtypeStruct((CH, ROWS, COLS), BF16),
            jax.ShapeDtypeStruct((3, 3, PART, CH), BF16),
            jax.ShapeDtypeStruct((CH, ROWS, COLS), BF16),
        ),
        in_specs=[vmem] * 4 + [whole] * 4,
        out_specs=(vmem,) * 3,
        scratch_shapes=[
            pltpu.VMEM((CH, ROWS, COLS), BF16),
            pltpu.VMEM((CH, ROWS, COLS), BF16),
            pltpu.VMEM((9 * CH, ALL), BF16),
            pltpu.VMEM((9 * CH, ALL), BF16),
            dma((4,)),
            pltpu.VMEM((ALL, LANES), BF16),
            pltpu.VMEM((ALL, LANES), BF16),
            pltpu.VMEM((ALL, LANES), BF16),
            pltpu.VMEM((3 * CH, CELLS), F32),
            pltpu.VMEM((CH, CELLS), F32),
            pltpu.VMEM((3 * CH, CELLS), BF16),
            pltpu.VMEM((CHANS, CH, 10 * CH), BF16),
            pltpu.VMEM((CHANS, CH, 10 * CH), BF16),
            pltpu.VMEM((10 * CH, ALL), BF16),
            pltpu.VMEM((TILES, PACK // 2, 128), BF16),
            pltpu.VMEM((4, 4, PACK // 2, 128), BF16),
            pltpu.VMEM((4, 4, PACK // 2, 128), BF16),
            pltpu.VMEM((ROWS * CH, TILES * CAP), BF16),
            pltpu.VMEM((2, 3, 96, ALL), BF16),
            pltpu.VMEM((3, 3, 96, ALL), BF16),
            pltpu.VMEM((3, 96, ALL), BF16),
            pltpu.VMEM((3, 3, 96, ALL), BF16),
            pltpu.VMEM((4, 2, 144, 128), BF16),
            pltpu.VMEM((144, 128), BF16),
            dma((3, 12)), dma((3, 12)), dma((3, 8)), dma((3, 8)), dma((3, 16)), dma((3, 16)),
            dma((2, 4)), dma((2, 4)), dma((CHANS,)), dma((CHANS,)), dma((4,)), dma((4,)),
            dma((2, 2)), dma((3, 2)), dma((2,)), dma((3, 2)), dma((4, 2)), dma((1,)),
        ],
        compiler_params=pltpu.CompilerParams(
            collective_id=0, has_side_effects=True, vmem_limit_bytes=56 * 1024 * 1024
        ),
    )(
        station_feats,
        owner_tile.reshape(1, SHARD),
        valid.reshape(1, SHARD),
        station_cell.reshape(1, SHARD),
        grad_out,
        grid,
        w1,
        w2,
    )
    return pl.pallas_call(
        hand_over,
        out_shape=tuple(jax.ShapeDtypeStruct(result.shape, result.dtype) for result in results),
        in_specs=[whole] * 3,
        out_specs=(whole,) * 3,
        scratch_shapes=[*(pltpu.VMEM(result.shape, BF16) for result in results), dma((2, 9))],
    )(*results)


def solution(mesh):
    return jax.shard_map(
        local,
        mesh=mesh,
        in_specs=(
            P("chan", "tile", None),
            P("chan", "tile"),
            P("tile", None),
            P("tile"),
            P("tile"),
            P(None, None, None, "chan"),
            P(None, None, None, "chan"),
            P("chan", "tile", None),
        ),
        out_specs=(P("chan", "tile", None), P(None, None, "tile", "chan"), P("chan", "tile", None)),
        check_vma=False,
    )
```

```python
import jax
import jax.numpy as jnp
from jax import lax
from jax.experimental import pallas as pl
from jax.experimental.pallas import tpu as pltpu
from jax.sharding import PartitionSpec as P

MESH = pl.DeviceIdType.MESH
BF16 = jnp.bfloat16
F32 = jnp.float32

CH = 64
ROWS = 16
COLS = 256
CELLS = ROWS * COLS
LANES = CELLS + 2 * COLS
BLOCK = CELLS // 2
TILES = 16
CHANS = 8
ALL = CH * CHANS
SHARD = 512
CAP = 64
PACK = 96
PART = 32
NT = (((1,), (1,)), ((), ()))

G, A, H = 0, 1, 2


def shifted(values, by):
    lanes = values.shape[1]
    col = lax.broadcasted_iota(jnp.int32, values.shape, 1) % COLS
    if by == 1:
        return jnp.where(col == 0, 0.0, pltpu.roll(values, 1, 1))
    return jnp.where(col == COLS - 1, 0.0, pltpu.roll(values, lanes - 1, 1))


def neighbour_sum(z):
    return z[CH : 2 * CH] + shifted(z[:CH], 1) + shifted(z[2 * CH :], -1)


def kernel(
    feats_ref, owner_ref, valid_ref, cell_ref, gout_hbm, grid_hbm, w1_hbm, w2_hbm,
    out_ref, gw_ref, gh_ref,
    gout_ref, grid_ref, w1_ref, w2_ref, in_sem, ga, aa, ha, zbuf, hidden_pre, h3, b2, wb, wbt, packed, passing, landed, masked,
    gw_out, gw_one, gw_mid, gw_two, gw_fin, gw_land,
    x_send, x_recv, e_send, e_recv, d_send, d_recv, s_send, s_recv, w_send, w_recv, u_send, u_recv, v_send, v_recv,
    one_send, one_recv, two_send, two_recv, three_send, three_recv,
):
    tile = lax.axis_index("tile")
    chan = lax.axis_index("chan")
    x, core = chan // 2, chan % 2
    y, z = tile // 4, tile % 4
    bufs = (ga, aa, ha)
    chips = [x, (x + 3) % 4, (x + 1) % 4, (x + 2) % 4]
    right = (tile, chips[2] * 2 + core)
    left = (tile, chips[1] * 2 + core)
    sibling = (tile, x * 2 + (1 - core))
    has_up, has_down = tile > 0, tile < TILES - 1

    inward = [
        pltpu.make_async_copy(src, dst, in_sem.at[k])
        for k, (src, dst) in enumerate(
            ((gout_hbm, gout_ref), (w2_hbm, w2_ref), (grid_hbm, grid_ref), (w1_hbm, w1_ref))
        )
    ]
    for copy in inward:
        copy.start()

    barrier = pltpu.get_barrier_semaphore()
    across_up, across_down = has_up & (z == 0), has_down & (z == 3)
    for step in range(1, 4):
        for peer in (y * 4 + (z + step) % 4, (y + step) % 4 * 4 + z):
            pl.semaphore_signal(barrier, inc=1, device_id=(peer, chan), device_id_type=MESH)
    for across, peer in ((across_up, jnp.maximum(tile - 1, 0)), (across_down, jnp.minimum(tile + 1, TILES - 1))):
        @pl.when(across)
        def _(peer=peer):
            pl.semaphore_signal(barrier, inc=1, device_id=(peer, chan), device_id_type=MESH)

    for step in range(1, CHANS):
        pl.semaphore_signal(barrier, inc=1, device_id=(tile, (chan + step) % CHANS), device_id_type=MESH)

    def rows_of(chip, which, low=0, size=CH):
        return pl.ds(pl.multiple_of(chip * (2 * CH) + which * CH + low, size), size)

    def pair_of(chip):
        return pl.ds(pl.multiple_of(chip * (2 * CH), 2 * CH), 2 * CH)

    own = rows_of(x, core)
    quarters = [pl.ds(COLS + q * 1024, 1024) for q in range(4)]
    middle = pl.ds(COLS + 1024, BLOCK)
    top, bottom = pl.ds(0, COLS), pl.ds(COLS + CELLS, COLS)
    first, last = pl.ds(COLS, COLS), pl.ds(CELLS, COLS)
    inner = pl.ds(COLS, CELLS)

    def remote(src, dst, send, recv, device):
        return pltpu.make_async_remote_copy(
            src_ref=src, dst_ref=dst, send_sem=send, recv_sem=recv, device_id=device, device_id_type=MESH
        )

    outer = (quarters[0], quarters[3], middle)
    x_table = (
        *((0, lanes, 0, CH, True, 1) for lanes in outer),
        *((0, lanes, 0, CH, False, 2) for lanes in outer),
        *((1, lanes, 0, CH // 2, True, 3) for lanes in outer),
        *((2, lanes, CH // 2, CH // 2, False, 3) for lanes in outer),
    )

    def x_copy(f, k, arriving=False):
        sent, lanes, low, size, to_right, received = x_table[k]
        place = bufs[f].at[rows_of(chips[received if arriving else sent], core, low, size), lanes]
        return remote(place, place, x_send.at[f, k], x_recv.at[f, k], right if to_right else left)

    def e_copy(f, j, down, arriving=False):
        rows = rows_of(chips[j], core)
        k = 2 * j + down
        src = bufs[f].at[rows, last if down else first]
        dst = bufs[f].at[rows, top if down else bottom]
        device = (jnp.minimum(tile + 1, TILES - 1) if down else jnp.maximum(tile - 1, 0), chan)
        return remote(dst if arriving else src, dst, e_send.at[f, k], e_recv.at[f, k], device)

    def e_start(f, j, down):
        @pl.when(has_down if down else has_up)
        def _():
            e_copy(f, j, down).start()

    def e_wait_recv(f, j, down):
        @pl.when(has_up if down else has_down)
        def _():
            e_copy(f, j, down, True).wait_recv()

    d_parts = (quarters[0], quarters[3], top, bottom, middle)
    d_table = ((0, pl.ds(0, LANES)), *((j, lanes) for j in (1, 2, 3) for lanes in d_parts))

    def d_copy(f, k, arriving=False):
        j, lanes = d_table[k]
        place = bufs[f].at[rows_of(chips[j], 1 - core if arriving else core), lanes]
        return remote(place, place, d_send.at[f, k], d_recv.at[f, k], sibling)

    def own_start(f, second):
        if second:
            x_copy(f, 2).start()
            x_copy(f, 5).start()
            return
        for k in (0, 3, 1, 4):
            x_copy(f, k).start()
        e_start(f, 0, 0)
        e_start(f, 0, 1)

    def pass_on(f, j):
        e_wait_recv(f, j, 1)
        if j:
            d_copy(f, 5 * j - 2).start()
        e_wait_recv(f, j, 0)
        d_copy(f, 5 * j - 1 if j else 0).start()

    def near_first(f, onward):
        for part in range(2):
            for side in range(2):
                x_copy(f, 3 * side + part, True).wait_recv()
                if onward:
                    x_copy(f, 6 + 3 * side + part).start()
                e_start(f, 1 + side, part)
                d_copy(f, 5 * side + 1 + part).start()

    def near_second(f, onward):
        for side in range(2):
            x_copy(f, 3 * side + 2, True).wait_recv()
            if onward:
                x_copy(f, 8 + 3 * side).start()
            d_copy(f, 5 * side + 5).start()

    def far_first(f):
        for part in range(2):
            x_copy(f, 6 + part, True).wait_recv()
            x_copy(f, 9 + part, True).wait_recv()
            e_start(f, 3, part)
            d_copy(f, 11 + part).start()

    def far_second(f):
        x_copy(f, 8, True).wait_recv()
        x_copy(f, 11, True).wait_recv()
        d_copy(f, 15).start()

    def far_edges(f):
        pass_on(f, 3)

    def d_wait(f, j):
        for k in range(len(d_table)):
            if d_table[k][0] == j:
                d_copy(f, k, True).wait_recv()

    def d_wait_parts(f, ks):
        for k in ks:
            d_copy(f, k, True).wait_recv()

    def products(buf, weights, pairs, start, size):
        total = None
        for r in range(3):
            lanes = pl.ds(start + r * COLS, size)
            taps = pl.ds(r * 3 * CH, 3 * CH)
            if pairs is None:
                lhs, rhs = weights[taps, :], buf[:, lanes]
            else:
                lhs = [weights[taps, pair_of(p)] for p in pairs]
                rhs = [buf[pair_of(p), lanes] for p in pairs]
                lhs = lhs[0] if len(lhs) == 1 else jnp.concatenate(lhs, axis=1)
                rhs = rhs[0] if len(rhs) == 1 else jnp.concatenate(rhs, axis=0)
            term = jnp.dot(lhs, rhs, preferred_element_type=F32)
            total = term if total is None else total + term
        return total

    def conv_pass(buf, weights, pairs, start):
        for block in range(2):
            lanes = pl.ds(block * BLOCK, BLOCK)
            terms = products(buf, weights, pairs, block * BLOCK, BLOCK)
            zbuf[:, lanes] = terms if start else zbuf[:, lanes] + terms

    with jax.named_scope("prepare"):
        inward[0].wait()
        ga[own, inner] = gout_ref[...].reshape(CH, CELLS)
        for buf in bufs:
            for chip in chips:
                @pl.when(tile == 0)
                def _(buf=buf, chip=chip):
                    buf[rows_of(chip, core), top] = jnp.zeros((CH, COLS), BF16)

                @pl.when(tile == TILES - 1)
                def _(buf=buf, chip=chip):
                    buf[rows_of(chip, core), bottom] = jnp.zeros((CH, COLS), BF16)

    with jax.named_scope("barrier_wait"):
        @pl.when(across_up | across_down)
        def _():
            pl.semaphore_wait(barrier, 6 + CHANS)

        @pl.when(jnp.logical_not(across_up | across_down))
        def _():
            pl.semaphore_wait(barrier, 6 + CHANS - 1)
    with jax.named_scope("first_sends"):
        own_start(G, 0)
        own_start(G, 1)

    with jax.named_scope("stations"):
        marks = jnp.concatenate([owner_ref[...], valid_ref[...], jnp.zeros((6, SHARD), jnp.int32)], axis=0)
        columns = marks.astype(F32).T
        owners, usable = columns[:, 0:1].astype(jnp.int32), columns[:, 1:2] == 1.0
        tile_of = lax.broadcasted_iota(jnp.int32, (SHARD, 128), 1)
        named = jnp.where((owners == tile_of) & usable, 1.0, 0.0)
        lower = lax.broadcasted_iota(jnp.int32, (SHARD, SHARD), 0) >= lax.broadcasted_iota(jnp.int32, (SHARD, SHARD), 1)
        counts = jnp.dot(jnp.where(lower, 1.0, 0.0).astype(BF16), named.astype(BF16), preferred_element_type=F32)
        rank = jnp.sum(counts * named, axis=1, keepdims=True).astype(jnp.int32) - 1
        slot = jnp.where(usable, owners * CAP + rank, -1)
        cells = cell_ref[...]
        sub = lax.broadcasted_iota(jnp.int32, (PACK - CH, SHARD), 0)
        places = jnp.where(sub == 0, cells // COLS, jnp.where(sub == 1, cells % COLS, 0))
        rowed = jnp.concatenate([feats_ref[...], places.astype(F32).astype(BF16)], axis=0)
        lane = lax.broadcasted_iota(jnp.int32, (PACK // 2, 128), 1)
        for part in range(2):
            number = lax.broadcasted_iota(jnp.int32, (SHARD, 512), 1) + part * 512
            chosen = jnp.where(slot == number, 1.0, 0.0).astype(BF16)
            sent = jnp.dot(rowed, chosen, preferred_element_type=F32)
            for k in range(4):
                upper, lower = sent[: PACK // 2, k * 128 : (k + 1) * 128], sent[PACK // 2 :, k * 128 : (k + 1) * 128]
                to = 2 * (part * 4 + k)
                packed[to % 4 * 4 + to // 4] = jnp.where(lane < CAP, upper, pltpu.roll(lower, CAP, 1)).astype(BF16)
                packed[(to + 1) % 4 * 4 + (to + 1) // 4] = jnp.where(lane < CAP, pltpu.roll(upper, CAP, 1), lower).astype(BF16)
        passing[z] = packed[pl.ds(z * 4, 4)]

    def s_copy(step, arriving=False):
        other = (z + step) % 4
        place = passing.at[(z + 4 - step) % 4]
        device = (y * 4 + other, chan)
        if arriving:
            return remote(place, place, s_send.at[0, step], s_recv.at[0, step], device)
        return remote(packed.at[pl.ds(other * 4, 4)], passing.at[z], s_send.at[0, step], s_recv.at[0, step], device)

    def t_copy(step, arriving=False):
        other = (y + step) % 4
        place = landed.at[(y + 4 - step) % 4]
        device = (other * 4 + z, chan)
        if arriving:
            return remote(place, place, s_send.at[1, step], s_recv.at[1, step], device)
        return remote(passing.at[:, other], landed.at[y], s_send.at[1, step], s_recv.at[1, step], device)

    z_rows = pl.ds(pl.multiple_of(z * 16, 16), 16)
    y_halves = (pl.ds(0, 384), pl.ds(384, 256))

    def by_half(act, turned=False):
        for half in range(2):
            @pl.when((y + turned) % 2 == half)
            def _(half=half):
                act(half)

    def w_copy(step, half, arriving=False):
        other = (chan + step) % CHANS
        lanes = y_halves[half]
        place = wb.at[(chan + CHANS - step) % CHANS, z_rows, lanes]
        if arriving:
            return remote(place, place, w_send.at[step], w_recv.at[step], (tile, other))
        return remote(b2.at[other, z_rows, lanes], wb.at[chan, z_rows, lanes], w_send.at[step], w_recv.at[step], (tile, other))

    def u_copy(half):
        place = wb.at[:, z_rows, y_halves[half]]
        return remote(place, place, u_send.at[0], u_recv.at[0], ((y + 1 - 2 * (y % 2)) * 4 + z, chan))

    def v_copy(step, arriving=False):
        other = y * 4 + (z + step) % 4
        quarter = (z + 4 - step) % 4 if arriving else z
        place = wb.at[:, pl.ds(pl.multiple_of(quarter * 16, 16), 16)]
        return remote(place, place, v_send.at[step], v_recv.at[step], (other, chan))

    for step in range(1, 4):
        s_copy(step).start()

    with jax.named_scope("weight_pieces"):
        inward[1].wait()
        lane = lax.broadcasted_iota(jnp.int32, (CH, 128), 1)
        for chip in range(4):
            taps = [w2_ref[pl.ds((8 - n) * CH, CH), pl.ds(chip * 128, 128)].astype(F32) for n in range(9)]
            turned = [pltpu.roll(tap, CH, 1) for tap in taps]
            for k in range(5):
                n = 2 * k
                even = jnp.where(lane < CH, taps[n], turned[n + 1] if n < 8 else 0.0)
                odd = jnp.where(lane < CH, turned[n], taps[n + 1] if n < 8 else 0.0)
                b2[2 * chip, :, pl.ds(k * 128, 128)] = even.astype(BF16)
                b2[2 * chip + 1, :, pl.ds(k * 128, 128)] = odd.astype(BF16)
        def weights_out(half):
            for step in range(1, CHANS):
                w_copy(step, half).start()
            wb[chan, z_rows, y_halves[half]] = b2[chan, z_rows, y_halves[half]]

        by_half(weights_out)

    with jax.named_scope("station_wait"):
        for step in range(1, 4):
            s_copy(step, True).wait_recv()
        for step in range(1, 4):
            t_copy(step).start()
        landed[y] = passing[:, y]
        for step in range(1, 4):
            t_copy(step, True).wait_recv()
    with jax.named_scope("assimilate"):
        lane = lax.broadcasted_iota(jnp.int32, (PACK // 2, 128), 1)
        slabs = []
        for k in range(TILES // 2):
            even, odd = landed[k // 2, k % 2 * 2].astype(F32), landed[k // 2, k % 2 * 2 + 1].astype(F32)
            upper = jnp.where(lane < CAP, even, pltpu.roll(odd, CAP, 1))
            lower = jnp.where(lane < CAP, pltpu.roll(even, CAP, 1), odd)
            slabs.append(jnp.concatenate([upper, lower], axis=0))
        stations = jnp.concatenate(slabs, axis=1)
        slots = stations.shape[1]
        station_row, station_col = stations[CH : CH + 1], stations[CH + 1 : CH + 2]
        spread = lax.broadcasted_iota(jnp.int32, (COLS, slots), 0).astype(F32)
        col_hot = jnp.where(station_col == spread, 1.0, 0.0).astype(BF16)
        features = stations[:CH]
        for i in range(ROWS):
            masked[pl.ds(i * CH, CH), :] = jnp.where(station_row == float(i), features, 0.0).astype(BF16)
        inward[2].wait()
        background = grid_ref[...].reshape(CH, CELLS)
        for number, quarter in enumerate((0, 3, 1, 2)):
            rows = pl.ds(quarter * 256, 256)
            sums = lax.dot_general(masked[rows, :], col_hot, NT, preferred_element_type=F32)
            for k in range(4):
                i = quarter * 4 + k
                value = background[:, i * COLS : (i + 1) * COLS].astype(F32) + sums[k * CH : (k + 1) * CH]
                aa[own, pl.ds((i + 1) * COLS, COLS)] = value.astype(BF16)
            if number % 2:
                own_start(A, number // 2)

    with jax.named_scope("pass_on_0"):
        pass_on(G, 0)
        pass_on(A, 0)
    with jax.named_scope("wait_A0"):
        d_wait(A, 0)
    with jax.named_scope("conv1_pass1"):
        inward[3].wait()
        conv_pass(aa, w1_ref, [chips[0]], True)
    with jax.named_scope("weights_round"):
        def weights_on(half):
            for step in range(1, CHANS):
                w_copy(step, half, True).wait_recv()
            u_copy(half).start()

        by_half(weights_on)
    with jax.named_scope("near_G1"):
        near_first(G, False)
    with jax.named_scope("near_A1"):
        near_first(A, True)
    with jax.named_scope("near_G2"):
        near_second(G, False)
        by_half(lambda half: u_copy(half).wait_recv(), True)
        for step in range(1, 4):
            v_copy(step).start()
    with jax.named_scope("near_A2"):
        near_second(A, True)
    with jax.named_scope("pass_on_A12"):
        pass_on(A, 1)
        pass_on(A, 2)
    with jax.named_scope("far_A1"):
        far_first(A)
    with jax.named_scope("wait_A12"):
        d_wait(A, 1)
        d_wait(A, 2)
    with jax.named_scope("conv1_pass2"):
        conv_pass(aa, w1_ref, [chips[1], chips[2]], False)
    with jax.named_scope("far_A2"):
        far_second(A)
        for k in (6, 9, 7, 10, 8, 11):
            x_copy(G, k).start()
    with jax.named_scope("far_A_edges"):
        far_edges(A)
        pass_on(G, 1)
        pass_on(G, 2)
    spans = ((0, 3 * COLS), (13 * COLS, 3 * COLS), (3 * COLS, 10 * COLS))

    with jax.named_scope("conv1_pass3"):
        d_wait_parts(A, (11, 12, 13, 14))
        for number, (start, size) in enumerate(spans):
            if number == 2:
                d_wait_parts(A, (15,))
            lanes = pl.ds(start, size)
            value = neighbour_sum(zbuf[:, lanes] + products(aa, w1_ref, [chips[3]], start, size))
            hidden_pre[:, lanes] = value
            hidden = value * (1.0 / (1.0 + jnp.exp(-value)))
            ha[own, pl.ds(start + COLS, size)] = hidden.astype(BF16)
        own_start(H, 0)

    groups = ((0, 1, 2), (3,))
    group_lanes = (pl.ds(0, 384), pl.ds(384, 128))

    def weight_terms(group):
        for r in range(3):
            lanes = pl.ds((2 - r) * COLS, CELLS)
            against = [ga[pair_of(chips[j]), lanes] for j in groups[group]]
            against = against[0] if len(against) == 1 else jnp.concatenate(against, axis=0)
            term = lax.dot_general(h3[...], against, NT, preferred_element_type=F32).astype(BF16)
            for part in range(2):
                gw_out[part, r, :, group_lanes[group]] = term[part * 96 : (part + 1) * 96]

    collects = z // 2 == core
    owns = collects & (y == x)

    def one_copy(part, group):
        target = 2 * core + part
        slot = jnp.maximum((target + 4 - z) % 4 - 1, 0)
        return remote(
            gw_out.at[part, :, :, group_lanes[group]],
            gw_one.at[slot, :, :, group_lanes[group]],
            one_send.at[part, group],
            one_recv.at[slot, group],
            (y * 4 + target, chan),
        )

    def one_start(group):
        for part in range(2):
            @pl.when(2 * core + part != z)
            def _(part=part):
                one_copy(part, group).start()

    def two_copy(group):
        slot = jnp.maximum((x + 4 - y) % 4 - 1, 0)
        return remote(
            gw_mid.at[:, :, group_lanes[group]],
            gw_two.at[slot, :, :, group_lanes[group]],
            two_send.at[group],
            two_recv.at[slot, group],
            (x * 4 + z, chan),
        )

    def slot_wait(buf, recv, slot, group):
        place = buf.at[slot, :, :, group_lanes[group]]
        remote(place, place, recv.at[slot, group], recv.at[slot, group], (tile, chan)).wait_recv()

    def collect(group):
        @pl.when(collects)
        def _():
            for slot in range(3):
                slot_wait(gw_one, one_recv, slot, group)
            lanes = group_lanes[group]
            total = gw_out[z % 2, :, :, lanes].astype(F32)
            for slot in range(3):
                total = total + gw_one[slot, :, :, lanes].astype(F32)
            gw_mid[:, :, lanes] = total.astype(BF16)

            @pl.when(y != x)
            def _():
                two_copy(group).start()

    def finish(group):
        @pl.when(owns)
        def _():
            for slot in range(3):
                slot_wait(gw_two, two_recv, slot, group)
            lanes = group_lanes[group]
            total = gw_mid[:, :, lanes].astype(F32)
            for slot in range(3):
                total = total + gw_two[slot, :, :, lanes].astype(F32)
            lane = lax.broadcasted_iota(jnp.int32, (144, 128), 1)
            for k, j in enumerate(groups[group]):
                both = total[:, :, k * 128 : (k + 1) * 128].reshape(288, 128)
                upper, lower = both[:144], both[144:]
                gw_fin[j, 0] = jnp.where(lane < CH, upper, pltpu.roll(lower, CH, 1)).astype(BF16)
                gw_fin[j, 1] = jnp.where(lane < CH, pltpu.roll(upper, CH, 1), lower).astype(BF16)
                for which in range(2):
                    if j == 0:
                        @pl.when(core != which)
                        def _(j=j, which=which):
                            three_copy(j, which).start()
                    else:
                        three_copy(j, which).start()
            if group == 0:
                gw_land[...] = gw_fin[0, core]

    def three_copy(j, which):
        return remote(
            gw_fin.at[j, which],
            gw_land,
            three_send.at[j, which],
            three_recv.at[0],
            (tile, chips[j] * 2 + which),
        )

    with jax.named_scope("hidden_columns"):
        mine_h = ha[own, inner].astype(F32)
        moved = (shifted(mine_h, 1), mine_h, shifted(mine_h, -1))
        for part in range(2):
            for q in range(3):
                h3[pl.ds(part * 96 + q * PART, PART), :] = moved[q][part * PART : (part + 1) * PART].astype(BF16)
    with jax.named_scope("weight_terms_0"):
        d_wait(G, 0)
        d_wait(G, 1)
        d_wait(G, 2)
        weight_terms(0)
    with jax.named_scope("pass_on_H0"):
        pass_on(H, 0)
    with jax.named_scope("far_G"):
        far_first(G)
        far_second(G)
        own_start(H, 1)
        one_start(0)
    with jax.named_scope("conv2_pass1"):
        d_wait(H, 0)
        conv_pass(ha, w2_ref, [chips[0]], True)
    with jax.named_scope("far_G_edges"):
        far_edges(G)
    with jax.named_scope("near_H1"):
        near_first(H, True)
    with jax.named_scope("weight_terms_1"):
        d_wait(G, 3)
        weight_terms(1)
        one_start(1)
    with jax.named_scope("turn_weights"):
        for step in range(1, 4):
            v_copy(step, True).wait_recv()
        for s in range(CHANS // 2):
            two = jnp.concatenate([wb[2 * s], wb[2 * s + 1]], axis=0).astype(F32)
            wbt[:, pl.ds(s * 128, 128)] = two.T.astype(BF16)
    def grad_hidden(block):
        lanes = pl.ds(block * BLOCK, BLOCK)
        grad_act = neighbour_sum(products(ga, wbt, None, block * BLOCK, BLOCK))
        value = hidden_pre[:, lanes]
        s = 1.0 / (1.0 + jnp.exp(-value))
        result = (grad_act * s * (1.0 + value * (1.0 - s))).astype(BF16)
        gh_ref[:, block * 8 : block * 8 + 8, :] = result.reshape(CH, 8, COLS)

    with jax.named_scope("grad_hidden_0"):
        grad_hidden(0)
    with jax.named_scope("collect_0"):
        collect(0)
    with jax.named_scope("near_H2"):
        near_second(H, True)
        pass_on(H, 1)
        pass_on(H, 2)
    with jax.named_scope("grad_hidden_1"):
        grad_hidden(1)
    with jax.named_scope("collect_1"):
        collect(1)
    with jax.named_scope("far_H1"):
        far_first(H)
    with jax.named_scope("conv2_pass2"):
        d_wait(H, 1)
        d_wait(H, 2)
        conv_pass(ha, w2_ref, [chips[1], chips[2]], False)
    with jax.named_scope("far_H2"):
        far_second(H)
    with jax.named_scope("far_H_edges"):
        far_edges(H)
    with jax.named_scope("finish_0"):
        finish(0)
    with jax.named_scope("finish_1"):
        finish(1)
    with jax.named_scope("conv2_pass3"):
        d_wait_parts(H, (11, 12, 13, 14))
        for number, (start, size) in enumerate(spans):
            if number == 2:
                d_wait_parts(H, (15,))
            lanes = pl.ds(start, size)
            branch = neighbour_sum(zbuf[:, lanes] + products(ha, w2_ref, [chips[3]], start, size))
            hidden_pre[:, lanes] = aa[own, pl.ds(start + COLS, size)].astype(F32) + branch
        out_ref[...] = hidden_pre[...].astype(BF16).reshape(CH, ROWS, COLS)
    with jax.named_scope("grad_weight"):
        @pl.when(jnp.logical_not(owns))
        def _():
            remote(gw_land, gw_land, three_recv.at[0], three_recv.at[0], (tile, chan)).wait_recv()

        piece = gw_land[...].astype(F32)
        sides = (piece[:, :CH].astype(BF16), pltpu.roll(piece, CH, 1)[:, :CH].astype(BF16))
        for n in range(18):
            rows = sides[n // 9][(n % 9) * 16 : (n % 9) * 16 + 16]
            gw_ref[n // 6, n % 6 // 2, pl.ds(n % 2 * 16, 16), :] = rows

    with jax.named_scope("sends_done"):
        for f in (G, A, H):
            for k in range(len(x_table)):
                x_copy(f, k).wait_send()
            for k in range(len(d_table)):
                d_copy(f, k).wait_send()
            for j in range(4):
                @pl.when(has_up)
                def _(f=f, j=j):
                    e_copy(f, j, 0).wait_send()

                @pl.when(has_down)
                def _(f=f, j=j):
                    e_copy(f, j, 1).wait_send()

        for step in range(1, 4):
            s_copy(step).wait_send()
            t_copy(step).wait_send()
        def weights_left(half):
            for step in range(1, CHANS):
                w_copy(step, half).wait_send()
            u_copy(half).wait_send()

        by_half(weights_left)
        for step in range(1, 4):
            v_copy(step).wait_send()
        for group in range(2):
            for part in range(2):
                @pl.when(2 * core + part != z)
                def _(part=part, group=group):
                    one_copy(part, group).wait_send()

            @pl.when(collects & (y != x))
            def _(group=group):
                two_copy(group).wait_send()

        @pl.when(owns)
        def _():
            for j in range(4):
                for which in range(2):
                    if j == 0:
                        @pl.when(core != which)
                        def _(j=j, which=which):
                            three_copy(j, which).wait_send()
                    else:
                        three_copy(j, which).wait_send()


def hand_over(out_from, gw_from, gh_from, out_to, gw_to, gh_to, out_via, gw_via, gh_via, sems):
    parts = [pl.ds(k * 16, 16) for k in range(4)]
    ways = [(gw_from, gw_via, gw_to)]
    for part in parts:
        ways.append((out_from.at[part], out_via.at[part], out_to.at[part]))
        ways.append((gh_from.at[part], gh_via.at[part], gh_to.at[part]))
    inward = [pltpu.make_async_copy(src, via, sems.at[0, k]) for k, (src, via, _) in enumerate(ways)]
    outward = [pltpu.make_async_copy(via, dst, sems.at[1, k]) for k, (_, via, dst) in enumerate(ways)]
    for copy in inward:
        copy.start()
    for arrive, leave in zip(inward, outward):
        arrive.wait()
        leave.start()
    for copy in outward:
        copy.wait()


def local(grid, station_feats, owner_tile, station_cell, valid, conv_first, conv_second, grad_out):
    w1 = conv_first.transpose(0, 1, 3, 2).reshape(9 * CH, ALL)
    w2 = conv_second.transpose(0, 1, 3, 2).reshape(9 * CH, ALL)
    whole = pl.BlockSpec(memory_space=pl.ANY)
    vmem = pl.BlockSpec(memory_space=pltpu.VMEM)
    dma = pltpu.SemaphoreType.DMA
    results = pl.pallas_call(
        kernel,
        out_shape=(
            jax.ShapeDtypeStruct((CH, ROWS, COLS), BF16),
            jax.ShapeDtypeStruct((3, 3, PART, CH), BF16),
            jax.ShapeDtypeStruct((CH, ROWS, COLS), BF16),
        ),
        in_specs=[vmem] * 4 + [whole] * 4,
        out_specs=(vmem,) * 3,
        scratch_shapes=[
            pltpu.VMEM((CH, ROWS, COLS), BF16),
            pltpu.VMEM((CH, ROWS, COLS), BF16),
            pltpu.VMEM((9 * CH, ALL), BF16),
            pltpu.VMEM((9 * CH, ALL), BF16),
            dma((4,)),
            pltpu.VMEM((ALL, LANES), BF16),
            pltpu.VMEM((ALL, LANES), BF16),
            pltpu.VMEM((ALL, LANES), BF16),
            pltpu.VMEM((3 * CH, CELLS), F32),
            pltpu.VMEM((CH, CELLS), F32),
            pltpu.VMEM((3 * CH, CELLS), BF16),
            pltpu.VMEM((CHANS, CH, 10 * CH), BF16),
            pltpu.VMEM((CHANS, CH, 10 * CH), BF16),
            pltpu.VMEM((10 * CH, ALL), BF16),
            pltpu.VMEM((TILES, PACK // 2, 128), BF16),
            pltpu.VMEM((4, 4, PACK // 2, 128), BF16),
            pltpu.VMEM((4, 4, PACK // 2, 128), BF16),
            pltpu.VMEM((ROWS * CH, TILES * CAP), BF16),
            pltpu.VMEM((2, 3, 96, ALL), BF16),
            pltpu.VMEM((3, 3, 96, ALL), BF16),
            pltpu.VMEM((3, 96, ALL), BF16),
            pltpu.VMEM((3, 3, 96, ALL), BF16),
            pltpu.VMEM((4, 2, 144, 128), BF16),
            pltpu.VMEM((144, 128), BF16),
            dma((3, 12)), dma((3, 12)), dma((3, 8)), dma((3, 8)), dma((3, 16)), dma((3, 16)),
            dma((2, 4)), dma((2, 4)), dma((CHANS,)), dma((CHANS,)), dma((1,)), dma((1,)), dma((4,)), dma((4,)),
            dma((2, 2)), dma((3, 2)), dma((2,)), dma((3, 2)), dma((4, 2)), dma((1,)),
        ],
        compiler_params=pltpu.CompilerParams(
            collective_id=0, has_side_effects=True, vmem_limit_bytes=56 * 1024 * 1024
        ),
    )(
        station_feats,
        owner_tile.reshape(1, SHARD),
        valid.reshape(1, SHARD),
        station_cell.reshape(1, SHARD),
        grad_out,
        grid,
        w1,
        w2,
    )
    return pl.pallas_call(
        hand_over,
        out_shape=tuple(jax.ShapeDtypeStruct(result.shape, result.dtype) for result in results),
        in_specs=[whole] * 3,
        out_specs=(whole,) * 3,
        scratch_shapes=[*(pltpu.VMEM(result.shape, BF16) for result in results), dma((2, 9))],
    )(*results)


def solution(mesh):
    return jax.shard_map(
        local,
        mesh=mesh,
        in_specs=(
            P("chan", "tile", None),
            P("chan", "tile"),
            P("tile", None),
            P("tile"),
            P("tile"),
            P(None, None, None, "chan"),
            P(None, None, None, "chan"),
            P("chan", "tile", None),
        ),
        out_specs=(P("chan", "tile", None), P(None, None, "tile", "chan"), P("chan", "tile", None)),
        check_vma=False,
    )
```

```python
import jax
import jax.numpy as jnp
from jax import lax
from jax.experimental import pallas as pl
from jax.experimental.pallas import tpu as pltpu
from jax.sharding import PartitionSpec as P

MESH = pl.DeviceIdType.MESH
BF16 = jnp.bfloat16
F32 = jnp.float32

CH = 64
ROWS = 16
COLS = 256
CELLS = ROWS * COLS
LANES = CELLS + 2 * COLS
BLOCK = CELLS // 2
TILES = 16
CHANS = 8
ALL = CH * CHANS
SHARD = 512
CAP = 64
PACK = 96
PART = 32
NT = (((1,), (1,)), ((), ()))

G, A, H = 0, 1, 2


def shifted(values, by):
    lanes = values.shape[1]
    col = lax.broadcasted_iota(jnp.int32, values.shape, 1) % COLS
    if by == 1:
        return jnp.where(col == 0, 0.0, pltpu.roll(values, 1, 1))
    return jnp.where(col == COLS - 1, 0.0, pltpu.roll(values, lanes - 1, 1))


def neighbour_sum(z):
    return z[CH : 2 * CH] + shifted(z[:CH], 1) + shifted(z[2 * CH :], -1)


def kernel(
    feats_ref, owner_ref, valid_ref, cell_ref, gout_hbm, grid_hbm, w1_hbm, w2_hbm,
    out_hbm, gw_hbm, gh_hbm,
    out_ref, gw_ref, gh_ref, out_sem,
    gout_ref, grid_ref, w1_ref, w2_ref, in_sem, ga, aa, ha, zbuf, hidden_pre, h3, b2, wb, wbt, packed, passing, landed, masked,
    gw_out, gw_one, gw_mid, gw_two, gw_fin, gw_land,
    x_send, x_recv, e_send, e_recv, d_send, d_recv, s_send, s_recv, w_send, w_recv, u_send, u_recv, v_send, v_recv,
    one_send, one_recv, two_send, two_recv, three_send, three_recv,
):
    tile = lax.axis_index("tile")
    chan = lax.axis_index("chan")
    x, core = chan // 2, chan % 2
    y, z = tile // 4, tile % 4
    bufs = (ga, aa, ha)
    chips = [x, (x + 3) % 4, (x + 1) % 4, (x + 2) % 4]
    right = (tile, chips[2] * 2 + core)
    left = (tile, chips[1] * 2 + core)
    sibling = (tile, x * 2 + (1 - core))
    has_up, has_down = tile > 0, tile < TILES - 1

    inward = [
        pltpu.make_async_copy(src, dst, in_sem.at[k])
        for k, (src, dst) in enumerate(
            ((gout_hbm, gout_ref), (w2_hbm, w2_ref), (grid_hbm, grid_ref), (w1_hbm, w1_ref))
        )
    ]
    for copy in inward:
        copy.start()
    outward = [
        pltpu.make_async_copy(src, dst, out_sem.at[k])
        for k, (src, dst) in enumerate(((gh_ref, gh_hbm), (out_ref, out_hbm), (gw_ref, gw_hbm)))
    ]

    barrier = pltpu.get_barrier_semaphore()
    across_up, across_down = has_up & (z == 0), has_down & (z == 3)
    for step in range(1, 4):
        for peer in (y * 4 + (z + step) % 4, (y + step) % 4 * 4 + z):
            pl.semaphore_signal(barrier, inc=1, device_id=(peer, chan), device_id_type=MESH)
    for across, peer in ((across_up, jnp.maximum(tile - 1, 0)), (across_down, jnp.minimum(tile + 1, TILES - 1))):
        @pl.when(across)
        def _(peer=peer):
            pl.semaphore_signal(barrier, inc=1, device_id=(peer, chan), device_id_type=MESH)

    for step in range(1, CHANS):
        pl.semaphore_signal(barrier, inc=1, device_id=(tile, (chan + step) % CHANS), device_id_type=MESH)

    def rows_of(chip, which, low=0, size=CH):
        return pl.ds(pl.multiple_of(chip * (2 * CH) + which * CH + low, size), size)

    def pair_of(chip):
        return pl.ds(pl.multiple_of(chip * (2 * CH), 2 * CH), 2 * CH)

    own = rows_of(x, core)
    quarters = [pl.ds(COLS + q * 1024, 1024) for q in range(4)]
    middle = pl.ds(COLS + 1024, BLOCK)
    top, bottom = pl.ds(0, COLS), pl.ds(COLS + CELLS, COLS)
    first, last = pl.ds(COLS, COLS), pl.ds(CELLS, COLS)
    inner = pl.ds(COLS, CELLS)

    def remote(src, dst, send, recv, device):
        return pltpu.make_async_remote_copy(
            src_ref=src, dst_ref=dst, send_sem=send, recv_sem=recv, device_id=device, device_id_type=MESH
        )

    outer = (quarters[0], quarters[3], middle)
    x_table = (
        *((0, lanes, 0, CH, True, 1) for lanes in outer),
        *((0, lanes, 0, CH, False, 2) for lanes in outer),
        *((1, lanes, 0, CH // 2, True, 3) for lanes in outer),
        *((2, lanes, CH // 2, CH // 2, False, 3) for lanes in outer),
    )

    def x_copy(f, k, arriving=False):
        sent, lanes, low, size, to_right, received = x_table[k]
        place = bufs[f].at[rows_of(chips[received if arriving else sent], core, low, size), lanes]
        return remote(place, place, x_send.at[f, k], x_recv.at[f, k], right if to_right else left)

    def e_copy(f, j, down, arriving=False):
        rows = rows_of(chips[j], core)
        k = 2 * j + down
        src = bufs[f].at[rows, last if down else first]
        dst = bufs[f].at[rows, top if down else bottom]
        device = (jnp.minimum(tile + 1, TILES - 1) if down else jnp.maximum(tile - 1, 0), chan)
        return remote(dst if arriving else src, dst, e_send.at[f, k], e_recv.at[f, k], device)

    def e_start(f, j, down):
        @pl.when(has_down if down else has_up)
        def _():
            e_copy(f, j, down).start()

    def e_wait_recv(f, j, down):
        @pl.when(has_up if down else has_down)
        def _():
            e_copy(f, j, down, True).wait_recv()

    d_parts = (quarters[0], quarters[3], top, bottom, middle)
    d_table = ((0, pl.ds(0, LANES)), *((j, lanes) for j in (1, 2, 3) for lanes in d_parts))

    def d_copy(f, k, arriving=False):
        j, lanes = d_table[k]
        place = bufs[f].at[rows_of(chips[j], 1 - core if arriving else core), lanes]
        return remote(place, place, d_send.at[f, k], d_recv.at[f, k], sibling)

    def own_start(f, second):
        if second:
            x_copy(f, 2).start()
            x_copy(f, 5).start()
            return
        for k in (0, 3, 1, 4):
            x_copy(f, k).start()
        e_start(f, 0, 0)
        e_start(f, 0, 1)

    def pass_on(f, j):
        e_wait_recv(f, j, 1)
        if j:
            d_copy(f, 5 * j - 2).start()
        e_wait_recv(f, j, 0)
        d_copy(f, 5 * j - 1 if j else 0).start()

    def near_first(f, onward):
        for part in range(2):
            for side in range(2):
                x_copy(f, 3 * side + part, True).wait_recv()
                if onward:
                    x_copy(f, 6 + 3 * side + part).start()
                e_start(f, 1 + side, part)
                d_copy(f, 5 * side + 1 + part).start()

    def near_second(f, onward):
        for side in range(2):
            x_copy(f, 3 * side + 2, True).wait_recv()
            if onward:
                x_copy(f, 8 + 3 * side).start()
            d_copy(f, 5 * side + 5).start()

    def far_first(f):
        for part in range(2):
            x_copy(f, 6 + part, True).wait_recv()
            x_copy(f, 9 + part, True).wait_recv()
            e_start(f, 3, part)
            d_copy(f, 11 + part).start()

    def far_second(f):
        x_copy(f, 8, True).wait_recv()
        x_copy(f, 11, True).wait_recv()
        d_copy(f, 15).start()

    def far_edges(f):
        pass_on(f, 3)

    def d_wait(f, j):
        for k in range(len(d_table)):
            if d_table[k][0] == j:
                d_copy(f, k, True).wait_recv()

    def d_wait_parts(f, ks):
        for k in ks:
            d_copy(f, k, True).wait_recv()

    def products(buf, weights, pairs, start, size):
        total = None
        for r in range(3):
            lanes = pl.ds(start + r * COLS, size)
            taps = pl.ds(r * 3 * CH, 3 * CH)
            if pairs is None:
                lhs, rhs = weights[taps, :], buf[:, lanes]
            else:
                lhs = [weights[taps, pair_of(p)] for p in pairs]
                rhs = [buf[pair_of(p), lanes] for p in pairs]
                lhs = lhs[0] if len(lhs) == 1 else jnp.concatenate(lhs, axis=1)
                rhs = rhs[0] if len(rhs) == 1 else jnp.concatenate(rhs, axis=0)
            term = jnp.dot(lhs, rhs, preferred_element_type=F32)
            total = term if total is None else total + term
        return total

    def conv_pass(buf, weights, pairs, start):
        for block in range(2):
            lanes = pl.ds(block * BLOCK, BLOCK)
            terms = products(buf, weights, pairs, block * BLOCK, BLOCK)
            zbuf[:, lanes] = terms if start else zbuf[:, lanes] + terms

    with jax.named_scope("prepare"):
        inward[0].wait()
        ga[own, inner] = gout_ref[...].reshape(CH, CELLS)
        for buf in bufs:
            for chip in chips:
                @pl.when(tile == 0)
                def _(buf=buf, chip=chip):
                    buf[rows_of(chip, core), top] = jnp.zeros((CH, COLS), BF16)

                @pl.when(tile == TILES - 1)
                def _(buf=buf, chip=chip):
                    buf[rows_of(chip, core), bottom] = jnp.zeros((CH, COLS), BF16)

    with jax.named_scope("barrier_wait"):
        @pl.when(across_up | across_down)
        def _():
            pl.semaphore_wait(barrier, 6 + CHANS)

        @pl.when(jnp.logical_not(across_up | across_down))
        def _():
            pl.semaphore_wait(barrier, 6 + CHANS - 1)
    with jax.named_scope("first_sends"):
        own_start(G, 0)
        own_start(G, 1)

    with jax.named_scope("stations"):
        marks = jnp.concatenate([owner_ref[...], valid_ref[...], jnp.zeros((6, SHARD), jnp.int32)], axis=0)
        columns = marks.astype(F32).T
        owners, usable = columns[:, 0:1].astype(jnp.int32), columns[:, 1:2] == 1.0
        tile_of = lax.broadcasted_iota(jnp.int32, (SHARD, 128), 1)
        named = jnp.where((owners == tile_of) & usable, 1.0, 0.0)
        lower = lax.broadcasted_iota(jnp.int32, (SHARD, SHARD), 0) >= lax.broadcasted_iota(jnp.int32, (SHARD, SHARD), 1)
        counts = jnp.dot(jnp.where(lower, 1.0, 0.0).astype(BF16), named.astype(BF16), preferred_element_type=F32)
        rank = jnp.sum(counts * named, axis=1, keepdims=True).astype(jnp.int32) - 1
        slot = jnp.where(usable, owners * CAP + rank, -1)
        cells = cell_ref[...]
        sub = lax.broadcasted_iota(jnp.int32, (PACK - CH, SHARD), 0)
        places = jnp.where(sub == 0, cells // COLS, jnp.where(sub == 1, cells % COLS, 0))
        rowed = jnp.concatenate([feats_ref[...], places.astype(F32).astype(BF16)], axis=0)
        lane = lax.broadcasted_iota(jnp.int32, (PACK // 2, 128), 1)
        for part in range(2):
            number = lax.broadcasted_iota(jnp.int32, (SHARD, 512), 1) + part * 512
            chosen = jnp.where(slot == number, 1.0, 0.0).astype(BF16)
            sent = jnp.dot(rowed, chosen, preferred_element_type=F32)
            for k in range(4):
                upper, lower = sent[: PACK // 2, k * 128 : (k + 1) * 128], sent[PACK // 2 :, k * 128 : (k + 1) * 128]
                to = 2 * (part * 4 + k)
                packed[to % 4 * 4 + to // 4] = jnp.where(lane < CAP, upper, pltpu.roll(lower, CAP, 1)).astype(BF16)
                packed[(to + 1) % 4 * 4 + (to + 1) // 4] = jnp.where(lane < CAP, pltpu.roll(upper, CAP, 1), lower).astype(BF16)
        passing[z] = packed[pl.ds(z * 4, 4)]

    def s_copy(step, arriving=False):
        other = (z + step) % 4
        place = passing.at[(z + 4 - step) % 4]
        device = (y * 4 + other, chan)
        if arriving:
            return remote(place, place, s_send.at[0, step], s_recv.at[0, step], device)
        return remote(packed.at[pl.ds(other * 4, 4)], passing.at[z], s_send.at[0, step], s_recv.at[0, step], device)

    def t_copy(step, arriving=False):
        other = (y + step) % 4
        place = landed.at[(y + 4 - step) % 4]
        device = (other * 4 + z, chan)
        if arriving:
            return remote(place, place, s_send.at[1, step], s_recv.at[1, step], device)
        return remote(passing.at[:, other], landed.at[y], s_send.at[1, step], s_recv.at[1, step], device)

    z_rows = pl.ds(pl.multiple_of(z * 16, 16), 16)
    y_halves = (pl.ds(0, 384), pl.ds(384, 256))

    def by_half(act, turned=False):
        for half in range(2):
            @pl.when((y + turned) % 2 == half)
            def _(half=half):
                act(half)

    def w_copy(step, half, arriving=False):
        other = (chan + step) % CHANS
        lanes = y_halves[half]
        place = wb.at[(chan + CHANS - step) % CHANS, z_rows, lanes]
        if arriving:
            return remote(place, place, w_send.at[step], w_recv.at[step], (tile, other))
        return remote(b2.at[other, z_rows, lanes], wb.at[chan, z_rows, lanes], w_send.at[step], w_recv.at[step], (tile, other))

    def u_copy(half):
        place = wb.at[:, z_rows, y_halves[half]]
        return remote(place, place, u_send.at[0], u_recv.at[0], ((y + 1 - 2 * (y % 2)) * 4 + z, chan))

    def v_copy(step, arriving=False):
        other = y * 4 + (z + step) % 4
        quarter = (z + 4 - step) % 4 if arriving else z
        place = wb.at[:, pl.ds(pl.multiple_of(quarter * 16, 16), 16)]
        return remote(place, place, v_send.at[step], v_recv.at[step], (other, chan))

    for step in range(1, 4):
        s_copy(step).start()

    with jax.named_scope("weight_pieces"):
        inward[1].wait()
        lane = lax.broadcasted_iota(jnp.int32, (CH, 128), 1)
        for chip in range(4):
            taps = [w2_ref[pl.ds((8 - n) * CH, CH), pl.ds(chip * 128, 128)].astype(F32) for n in range(9)]
            turned = [pltpu.roll(tap, CH, 1) for tap in taps]
            for k in range(5):
                n = 2 * k
                even = jnp.where(lane < CH, taps[n], turned[n + 1] if n < 8 else 0.0)
                odd = jnp.where(lane < CH, turned[n], taps[n + 1] if n < 8 else 0.0)
                b2[2 * chip, :, pl.ds(k * 128, 128)] = even.astype(BF16)
                b2[2 * chip + 1, :, pl.ds(k * 128, 128)] = odd.astype(BF16)
        def weights_out(half):
            for step in range(1, CHANS):
                w_copy(step, half).start()
            wb[chan, z_rows, y_halves[half]] = b2[chan, z_rows, y_halves[half]]

        by_half(weights_out)

    with jax.named_scope("station_wait"):
        for step in range(1, 4):
            s_copy(step, True).wait_recv()
        for step in range(1, 4):
            t_copy(step).start()
        landed[y] = passing[:, y]
        for step in range(1, 4):
            t_copy(step, True).wait_recv()
    with jax.named_scope("assimilate"):
        lane = lax.broadcasted_iota(jnp.int32, (PACK // 2, 128), 1)
        slabs = []
        for k in range(TILES // 2):
            even, odd = landed[k // 2, k % 2 * 2].astype(F32), landed[k // 2, k % 2 * 2 + 1].astype(F32)
            upper = jnp.where(lane < CAP, even, pltpu.roll(odd, CAP, 1))
            lower = jnp.where(lane < CAP, pltpu.roll(even, CAP, 1), odd)
            slabs.append(jnp.concatenate([upper, lower], axis=0))
        stations = jnp.concatenate(slabs, axis=1)
        slots = stations.shape[1]
        station_row, station_col = stations[CH : CH + 1], stations[CH + 1 : CH + 2]
        spread = lax.broadcasted_iota(jnp.int32, (COLS, slots), 0).astype(F32)
        col_hot = jnp.where(station_col == spread, 1.0, 0.0).astype(BF16)
        features = stations[:CH]
        for i in range(ROWS):
            masked[pl.ds(i * CH, CH), :] = jnp.where(station_row == float(i), features, 0.0).astype(BF16)
        inward[2].wait()
        background = grid_ref[...].reshape(CH, CELLS)
        for number, quarter in enumerate((0, 3, 1, 2)):
            rows = pl.ds(quarter * 256, 256)
            sums = lax.dot_general(masked[rows, :], col_hot, NT, preferred_element_type=F32)
            for k in range(4):
                i = quarter * 4 + k
                value = background[:, i * COLS : (i + 1) * COLS].astype(F32) + sums[k * CH : (k + 1) * CH]
                aa[own, pl.ds((i + 1) * COLS, COLS)] = value.astype(BF16)
            if number % 2:
                own_start(A, number // 2)

    with jax.named_scope("pass_on_0"):
        pass_on(G, 0)
        pass_on(A, 0)
    with jax.named_scope("wait_A0"):
        d_wait(A, 0)
    with jax.named_scope("conv1_pass1"):
        inward[3].wait()
        conv_pass(aa, w1_ref, [chips[0]], True)
    with jax.named_scope("weights_round"):
        def weights_on(half):
            for step in range(1, CHANS):
                w_copy(step, half, True).wait_recv()
            u_copy(half).start()

        by_half(weights_on)
    with jax.named_scope("near_G1"):
        near_first(G, False)
    with jax.named_scope("near_A1"):
        near_first(A, True)
    with jax.named_scope("near_G2"):
        near_second(G, False)
        by_half(lambda half: u_copy(half).wait_recv(), True)
        for step in range(1, 4):
            v_copy(step).start()
    with jax.named_scope("near_A2"):
        near_second(A, True)
    with jax.named_scope("pass_on_A12"):
        pass_on(A, 1)
        pass_on(A, 2)
    with jax.named_scope("far_A1"):
        far_first(A)
    with jax.named_scope("wait_A12"):
        d_wait(A, 1)
        d_wait(A, 2)
    with jax.named_scope("conv1_pass2"):
        conv_pass(aa, w1_ref, [chips[1], chips[2]], False)
    with jax.named_scope("far_A2"):
        far_second(A)
        for k in (6, 9, 7, 10, 8, 11):
            x_copy(G, k).start()
    with jax.named_scope("far_A_edges"):
        far_edges(A)
        pass_on(G, 1)
        pass_on(G, 2)
    spans = ((0, 3 * COLS), (13 * COLS, 3 * COLS), (3 * COLS, 10 * COLS))

    with jax.named_scope("conv1_pass3"):
        d_wait_parts(A, (11, 12, 13, 14))
        for number, (start, size) in enumerate(spans):
            if number == 2:
                d_wait_parts(A, (15,))
            lanes = pl.ds(start, size)
            value = neighbour_sum(zbuf[:, lanes] + products(aa, w1_ref, [chips[3]], start, size))
            hidden_pre[:, lanes] = value
            hidden = value * (1.0 / (1.0 + jnp.exp(-value)))
            ha[own, pl.ds(start + COLS, size)] = hidden.astype(BF16)
        own_start(H, 0)

    groups = ((0, 1, 2), (3,))
    group_lanes = (pl.ds(0, 384), pl.ds(384, 128))

    def weight_terms(group):
        for r in range(3):
            lanes = pl.ds((2 - r) * COLS, CELLS)
            against = [ga[pair_of(chips[j]), lanes] for j in groups[group]]
            against = against[0] if len(against) == 1 else jnp.concatenate(against, axis=0)
            term = lax.dot_general(h3[...], against, NT, preferred_element_type=F32).astype(BF16)
            for part in range(2):
                gw_out[part, r, :, group_lanes[group]] = term[part * 96 : (part + 1) * 96]

    collects = z // 2 == core
    owns = collects & (y == x)

    def one_copy(part, group):
        target = 2 * core + part
        slot = jnp.maximum((target + 4 - z) % 4 - 1, 0)
        return remote(
            gw_out.at[part, :, :, group_lanes[group]],
            gw_one.at[slot, :, :, group_lanes[group]],
            one_send.at[part, group],
            one_recv.at[slot, group],
            (y * 4 + target, chan),
        )

    def one_start(group):
        for part in range(2):
            @pl.when(2 * core + part != z)
            def _(part=part):
                one_copy(part, group).start()

    def two_copy(group):
        slot = jnp.maximum((x + 4 - y) % 4 - 1, 0)
        return remote(
            gw_mid.at[:, :, group_lanes[group]],
            gw_two.at[slot, :, :, group_lanes[group]],
            two_send.at[group],
            two_recv.at[slot, group],
            (x * 4 + z, chan),
        )

    def slot_wait(buf, recv, slot, group):
        place = buf.at[slot, :, :, group_lanes[group]]
        remote(place, place, recv.at[slot, group], recv.at[slot, group], (tile, chan)).wait_recv()

    def collect(group):
        @pl.when(collects)
        def _():
            for slot in range(3):
                slot_wait(gw_one, one_recv, slot, group)
            lanes = group_lanes[group]
            total = gw_out[z % 2, :, :, lanes].astype(F32)
            for slot in range(3):
                total = total + gw_one[slot, :, :, lanes].astype(F32)
            gw_mid[:, :, lanes] = total.astype(BF16)

            @pl.when(y != x)
            def _():
                two_copy(group).start()

    def finish(group):
        @pl.when(owns)
        def _():
            for slot in range(3):
                slot_wait(gw_two, two_recv, slot, group)
            lanes = group_lanes[group]
            total = gw_mid[:, :, lanes].astype(F32)
            for slot in range(3):
                total = total + gw_two[slot, :, :, lanes].astype(F32)
            lane = lax.broadcasted_iota(jnp.int32, (144, 128), 1)
            for k, j in enumerate(groups[group]):
                both = total[:, :, k * 128 : (k + 1) * 128].reshape(288, 128)
                upper, lower = both[:144], both[144:]
                gw_fin[j, 0] = jnp.where(lane < CH, upper, pltpu.roll(lower, CH, 1)).astype(BF16)
                gw_fin[j, 1] = jnp.where(lane < CH, pltpu.roll(upper, CH, 1), lower).astype(BF16)
                for which in range(2):
                    if j == 0:
                        @pl.when(core != which)
                        def _(j=j, which=which):
                            three_copy(j, which).start()
                    else:
                        three_copy(j, which).start()
            if group == 0:
                gw_land[...] = gw_fin[0, core]

    def three_copy(j, which):
        return remote(
            gw_fin.at[j, which],
            gw_land,
            three_send.at[j, which],
            three_recv.at[0],
            (tile, chips[j] * 2 + which),
        )

    with jax.named_scope("hidden_columns"):
        mine_h = ha[own, inner].astype(F32)
        moved = (shifted(mine_h, 1), mine_h, shifted(mine_h, -1))
        for part in range(2):
            for q in range(3):
                h3[pl.ds(part * 96 + q * PART, PART), :] = moved[q][part * PART : (part + 1) * PART].astype(BF16)
    with jax.named_scope("weight_terms_0"):
        d_wait(G, 0)
        d_wait(G, 1)
        d_wait(G, 2)
        weight_terms(0)
    with jax.named_scope("pass_on_H0"):
        pass_on(H, 0)
    with jax.named_scope("far_G"):
        far_first(G)
        far_second(G)
        own_start(H, 1)
        one_start(0)
    with jax.named_scope("conv2_pass1"):
        d_wait(H, 0)
        conv_pass(ha, w2_ref, [chips[0]], True)
    with jax.named_scope("far_G_edges"):
        far_edges(G)
    with jax.named_scope("near_H1"):
        near_first(H, True)
    with jax.named_scope("weight_terms_1"):
        d_wait(G, 3)
        weight_terms(1)
        one_start(1)
    with jax.named_scope("turn_weights"):
        for step in range(1, 4):
            v_copy(step, True).wait_recv()
        for s in range(CHANS // 2):
            two = jnp.concatenate([wb[2 * s], wb[2 * s + 1]], axis=0).astype(F32)
            wbt[:, pl.ds(s * 128, 128)] = two.T.astype(BF16)
    def grad_hidden(block):
        lanes = pl.ds(block * BLOCK, BLOCK)
        grad_act = neighbour_sum(products(ga, wbt, None, block * BLOCK, BLOCK))
        value = hidden_pre[:, lanes]
        s = 1.0 / (1.0 + jnp.exp(-value))
        result = (grad_act * s * (1.0 + value * (1.0 - s))).astype(BF16)
        gh_ref[:, block * 8 : block * 8 + 8, :] = result.reshape(CH, 8, COLS)

    with jax.named_scope("grad_hidden_0"):
        grad_hidden(0)
    with jax.named_scope("collect_0"):
        collect(0)
    with jax.named_scope("near_H2"):
        near_second(H, True)
        pass_on(H, 1)
        pass_on(H, 2)
    with jax.named_scope("grad_hidden_1"):
        grad_hidden(1)
        outward[0].start()
    with jax.named_scope("collect_1"):
        collect(1)
    with jax.named_scope("far_H1"):
        far_first(H)
    with jax.named_scope("conv2_pass2"):
        d_wait(H, 1)
        d_wait(H, 2)
        conv_pass(ha, w2_ref, [chips[1], chips[2]], False)
    with jax.named_scope("far_H2"):
        far_second(H)
    with jax.named_scope("far_H_edges"):
        far_edges(H)
    with jax.named_scope("finish_0"):
        finish(0)
    with jax.named_scope("finish_1"):
        finish(1)
    with jax.named_scope("conv2_pass3"):
        d_wait_parts(H, (11, 12, 13, 14))
        for number, (start, size) in enumerate(spans):
            if number == 2:
                d_wait_parts(H, (15,))
            lanes = pl.ds(start, size)
            branch = neighbour_sum(zbuf[:, lanes] + products(ha, w2_ref, [chips[3]], start, size))
            hidden_pre[:, lanes] = aa[own, pl.ds(start + COLS, size)].astype(F32) + branch
        out_ref[...] = hidden_pre[...].astype(BF16).reshape(CH, ROWS, COLS)
        outward[1].start()
    with jax.named_scope("grad_weight"):
        @pl.when(jnp.logical_not(owns))
        def _():
            remote(gw_land, gw_land, three_recv.at[0], three_recv.at[0], (tile, chan)).wait_recv()

        piece = gw_land[...].astype(F32)
        sides = (piece[:, :CH].astype(BF16), pltpu.roll(piece, CH, 1)[:, :CH].astype(BF16))
        for n in range(18):
            rows = sides[n // 9][(n % 9) * 16 : (n % 9) * 16 + 16]
            gw_ref[n // 6, n % 6 // 2, pl.ds(n % 2 * 16, 16), :] = rows

        outward[2].start()

    with jax.named_scope("sends_done"):
        for f in (G, A, H):
            for k in range(len(x_table)):
                x_copy(f, k).wait_send()
            for k in range(len(d_table)):
                d_copy(f, k).wait_send()
            for j in range(4):
                @pl.when(has_up)
                def _(f=f, j=j):
                    e_copy(f, j, 0).wait_send()

                @pl.when(has_down)
                def _(f=f, j=j):
                    e_copy(f, j, 1).wait_send()

        for step in range(1, 4):
            s_copy(step).wait_send()
            t_copy(step).wait_send()
        def weights_left(half):
            for step in range(1, CHANS):
                w_copy(step, half).wait_send()
            u_copy(half).wait_send()

        by_half(weights_left)
        for step in range(1, 4):
            v_copy(step).wait_send()
        for group in range(2):
            for part in range(2):
                @pl.when(2 * core + part != z)
                def _(part=part, group=group):
                    one_copy(part, group).wait_send()

            @pl.when(collects & (y != x))
            def _(group=group):
                two_copy(group).wait_send()

        @pl.when(owns)
        def _():
            for j in range(4):
                for which in range(2):
                    if j == 0:
                        @pl.when(core != which)
                        def _(j=j, which=which):
                            three_copy(j, which).wait_send()
                    else:
                        three_copy(j, which).wait_send()
        for copy in outward:
            copy.wait()


def hand_over(out_from, gw_from, gh_from, out_to, gw_to, gh_to, out_via, gw_via, gh_via, sems):
    parts = [pl.ds(k * 16, 16) for k in range(4)]
    ways = [(gw_from, gw_via, gw_to)]
    for part in parts:
        ways.append((out_from.at[part], out_via.at[part], out_to.at[part]))
        ways.append((gh_from.at[part], gh_via.at[part], gh_to.at[part]))
    inward = [pltpu.make_async_copy(src, via, sems.at[0, k]) for k, (src, via, _) in enumerate(ways)]
    outward = [pltpu.make_async_copy(via, dst, sems.at[1, k]) for k, (_, via, dst) in enumerate(ways)]
    for copy in inward:
        copy.start()
    for arrive, leave in zip(inward, outward):
        arrive.wait()
        leave.start()
    for copy in outward:
        copy.wait()


def local(grid, station_feats, owner_tile, station_cell, valid, conv_first, conv_second, grad_out):
    w1 = conv_first.transpose(0, 1, 3, 2).reshape(9 * CH, ALL)
    w2 = conv_second.transpose(0, 1, 3, 2).reshape(9 * CH, ALL)
    whole = pl.BlockSpec(memory_space=pl.ANY)
    vmem = pl.BlockSpec(memory_space=pltpu.VMEM)
    dma = pltpu.SemaphoreType.DMA
    results = pl.pallas_call(
        kernel,
        out_shape=(
            jax.ShapeDtypeStruct((CH, ROWS, COLS), BF16),
            jax.ShapeDtypeStruct((3, 3, PART, CH), BF16),
            jax.ShapeDtypeStruct((CH, ROWS, COLS), BF16),
        ),
        in_specs=[vmem] * 4 + [whole] * 4,
        out_specs=(whole,) * 3,
        scratch_shapes=[
            pltpu.VMEM((CH, ROWS, COLS), BF16),
            pltpu.VMEM((3, 3, PART, CH), BF16),
            pltpu.VMEM((CH, ROWS, COLS), BF16),
            dma((3,)),
            pltpu.VMEM((CH, ROWS, COLS), BF16),
            pltpu.VMEM((CH, ROWS, COLS), BF16),
            pltpu.VMEM((9 * CH, ALL), BF16),
            pltpu.VMEM((9 * CH, ALL), BF16),
            dma((4,)),
            pltpu.VMEM((ALL, LANES), BF16),
            pltpu.VMEM((ALL, LANES), BF16),
            pltpu.VMEM((ALL, LANES), BF16),
            pltpu.VMEM((3 * CH, CELLS), F32),
            pltpu.VMEM((CH, CELLS), F32),
            pltpu.VMEM((3 * CH, CELLS), BF16),
            pltpu.VMEM((CHANS, CH, 10 * CH), BF16),
            pltpu.VMEM((CHANS, CH, 10 * CH), BF16),
            pltpu.VMEM((10 * CH, ALL), BF16),
            pltpu.VMEM((TILES, PACK // 2, 128), BF16),
            pltpu.VMEM((4, 4, PACK // 2, 128), BF16),
            pltpu.VMEM((4, 4, PACK // 2, 128), BF16),
            pltpu.VMEM((ROWS * CH, TILES * CAP), BF16),
            pltpu.VMEM((2, 3, 96, ALL), BF16),
            pltpu.VMEM((3, 3, 96, ALL), BF16),
            pltpu.VMEM((3, 96, ALL), BF16),
            pltpu.VMEM((3, 3, 96, ALL), BF16),
            pltpu.VMEM((4, 2, 144, 128), BF16),
            pltpu.VMEM((144, 128), BF16),
            dma((3, 12)), dma((3, 12)), dma((3, 8)), dma((3, 8)), dma((3, 16)), dma((3, 16)),
            dma((2, 4)), dma((2, 4)), dma((CHANS,)), dma((CHANS,)), dma((1,)), dma((1,)), dma((4,)), dma((4,)),
            dma((2, 2)), dma((3, 2)), dma((2,)), dma((3, 2)), dma((4, 2)), dma((1,)),
        ],
        compiler_params=pltpu.CompilerParams(
            collective_id=0, has_side_effects=True, vmem_limit_bytes=56 * 1024 * 1024
        ),
    )(
        station_feats,
        owner_tile.reshape(1, SHARD),
        valid.reshape(1, SHARD),
        station_cell.reshape(1, SHARD),
        grad_out,
        grid,
        w1,
        w2,
    )
    return pl.pallas_call(
        hand_over,
        out_shape=tuple(jax.ShapeDtypeStruct(result.shape, result.dtype) for result in results),
        in_specs=[whole] * 3,
        out_specs=(whole,) * 3,
        scratch_shapes=[*(pltpu.VMEM(result.shape, BF16) for result in results), dma((2, 9))],
    )(*results)


def solution(mesh):
    return jax.shard_map(
        local,
        mesh=mesh,
        in_specs=(
            P("chan", "tile", None),
            P("chan", "tile"),
            P("tile", None),
            P("tile"),
            P("tile"),
            P(None, None, None, "chan"),
            P(None, None, None, "chan"),
            P("chan", "tile", None),
        ),
        out_specs=(P("chan", "tile", None), P(None, None, "tile", "chan"), P("chan", "tile", None)),
        check_vma=False,
    )
```
